32 devices in a mesh: grp: 2 (over x), scan: 8 (over z, y), det: 2 (over core).
Axes of the slice: x: 2, y: 2, z: 4, core: 2. Of those that a mesh axis runs over, the one named last changes fastest.
Arguments:
- spectra: float32 [16384, 4096], P(('grp', 'scan'), 'det'), parts along dimension 0, may hold values from 0 to 544, as said below
- basis: float32 [64, 4096], P('grp', 'det'), parts along dimension 0, may hold values from 0.03 to 8, as said below
- loadings: float32 [64, 8192], P('grp', 'scan'), parts along dimension 0, may hold values from 0.005 to 6, as said below
Outputs:
- new_loadings: float32 [64, 8192], P('grp', 'scan'), parts along dimension 0
- new_basis: float32 [64, 4096], P('grp', 'det'), parts along dimension 0
The draws below stay inside these ranges and needn't reach their ends.
There are 2 independent parts, one for each index of `grp`. The reference program is written for one: setup_inputs(seed, part) draws one part's arguments, and reference() takes and returns one part's arrays. A program takes and returns all parts, laid end to end along the dimension named above; each array names one. Nothing has to cross between parts.
Inputs may be any that keep to these rules, and one draw needn't show every extreme that they name: `spectra`: intensities are nonnegative. `basis`: entries are positive. `loadings`: entries are positive.
All inputs are finite; a program needn't handle non-finite values.
Results may differ from the reference program's by a relative error of at most 0.00005.
Values sent between devices are 32-bit elements; how exact they have to be, the bound alone decides.
No kernel may reach another device: no remote copies, remote signals or barrier semaphores. Data moves between devices by JAX's collectives and lax.ppermute only.
A program may use at most 64 MiB of HBM per device.

```python
import math
import jax
import jax.numpy as jnp
from jax import lax

Q = 4096
R = 32
POSITIONS = 8192


def truth(key):
    side = math.isqrt(Q)
    cell = jnp.arange(Q, dtype=jnp.int32)
    row_pos = (cell // side).astype(jnp.float32)
    col_pos = (cell % side).astype(jnp.float32)
    key_center = jax.random.fold_in(key, 101)
    key_radius = jax.random.fold_in(key, 102)
    key_amp = jax.random.fold_in(key, 103)
    key_gain = jax.random.fold_in(key, 104)
    key_block = jax.random.fold_in(key, 105)
    key_entry = jax.random.fold_in(key, 106)
    centers = jax.random.uniform(key_center, (R, 2), jnp.float32, 0.0, side - 1.0)
    radius = side * jax.random.uniform(key_radius, (R, 1), jnp.float32, 0.06, 0.2)
    amplitude = jax.random.uniform(key_amp, (R, 1), jnp.float32, 1.0, 2.0)
    gain = jax.random.uniform(key_gain, (Q,), jnp.float32, 0.5, 1.5)
    background = 0.15
    row_off = row_pos[None, :] - centers[:, 0:1]
    col_off = col_pos[None, :] - centers[:, 1:2]
    dist = row_off * row_off + col_off * col_off
    pattern = (background + amplitude * jnp.exp(-dist / (2.0 * radius * radius))) * gain[None, :]
    block_count = POSITIONS // 16
    block_scale = jnp.exp(jax.random.uniform(key_block, (R, block_count), jnp.float32, math.log(0.02), math.log(2.0)))
    entry = jax.random.uniform(key_entry, (R, POSITIONS), jnp.float32, 0.5, 1.5)
    abundance = jnp.repeat(block_scale, 16, axis=1) * entry
    return (pattern, abundance)


def draw_spectra(key, part):
    pattern, abundance = truth(key)
    clean = jnp.dot(abundance.T, pattern, precision=lax.Precision.HIGHEST)
    key_noise = jax.random.fold_in(key, 201)
    key_offset = jax.random.fold_in(key, 202)
    factor = jax.random.uniform(key_noise, (POSITIONS, Q), jnp.float32, 0.6, 1.4)
    offset = jax.random.uniform(key_offset, (POSITIONS, Q), jnp.float32, 0.0, 0.5)
    return clean * factor + offset


def draw_basis(key, part):
    pattern, abundance = truth(key)
    key_noise = jax.random.fold_in(key, 301)
    factor = jnp.exp(jax.random.uniform(key_noise, (R, Q), jnp.float32, math.log(0.5), math.log(2.0)))
    return pattern * factor


def draw_loadings(key, part):
    pattern, abundance = truth(key)
    key_noise = jax.random.fold_in(key, 401)
    factor = jnp.exp(jax.random.uniform(key_noise, (R, POSITIONS), jnp.float32, math.log(0.5), math.log(2.0)))
    return abundance * factor


def setup_inputs(seed: int = 0, part: int = 0) -> dict:
    splits = jax.random.split(jax.random.key(seed), 4)
    part_splits = jax.random.split(jax.random.fold_in(splits[3], part), 4)
    spectra = draw_spectra(jax.random.fold_in(jax.random.fold_in(splits[3], part), 71), part)
    basis = draw_basis(jax.random.fold_in(jax.random.fold_in(splits[3], part), 71), part)
    loadings = draw_loadings(jax.random.fold_in(jax.random.fold_in(splits[3], part), 71), part)
    return dict(spectra=spectra, basis=basis, loadings=loadings)


HIGHEST = lax.Precision.HIGHEST


def reference(spectra, basis, loadings):
    tied = 0.5 * (basis + jnp.flip(basis, 1))
    numer_h = lax.dot_general(tied, spectra, (((1,), (1,)), ((), ())), precision=HIGHEST)
    gram = lax.dot_general(tied, tied, (((1,), (1,)), ((), ())), precision=HIGHEST)
    new_loadings = loadings * numer_h / jnp.dot(gram, loadings, precision=HIGHEST)
    numer_w = jnp.dot(new_loadings, spectra, precision=HIGHEST)
    cross = lax.dot_general(new_loadings, new_loadings, (((1,), (1,)), ((), ())), precision=HIGHEST)
    tied_numer = 0.5 * (numer_w + jnp.flip(numer_w, 1))
    new_basis = tied * tied_numer / jnp.dot(cross, tied, precision=HIGHEST)
    return new_loadings, new_basis
```

```python
import functools

import jax
import jax.numpy as jnp
from jax import lax
from jax.experimental import pallas as pl
from jax.experimental.pallas import tpu as pltpu
from jax.sharding import PartitionSpec as P

HIGHEST = lax.Precision.HIGHEST
LANES = 128
MIB = 1 << 20
F32, BF16 = jnp.float32, jnp.bfloat16
NT = (((1,), (1,)), ((), ()))
NN = (((1,), (0,)), ((), ()))


def in_vmem(x):
    return pltpu.with_memory_space_constraint(x, pltpu.VMEM)


def vmem_specs(count):
    return [pl.BlockSpec(memory_space=pltpu.VMEM)] * count


def halves(x):
    high = x.astype(BF16)
    return high, (x - high.astype(F32)).astype(BF16)


def mirror_lanes(block):
    lane = lax.broadcasted_iota(jnp.int32, block.shape, 1)
    return jnp.take_along_axis(block, LANES - 1 - lane, axis=1, mode="promise_in_bounds")


def dot(a, b, dims, precision=None):
    return lax.dot_general(a, b, dims, precision=precision, preferred_element_type=F32)


def numer_kernel(rows, spectra, basis, partner, loadings, numer, ratio, tied, high, low, stage, sems):
    rank, cols = basis.shape
    chunks = spectra.shape[0] // rows
    copies = [
        pltpu.make_async_copy(spectra.at[pl.ds(i * rows, rows)], stage.at[pl.ds(i * rows, rows)], sems.at[i])
        for i in range(chunks)
    ]
    for copy in copies:
        copy.start()
    blocks = cols // LANES
    for j in range(blocks):
        mirrored = mirror_lanes(partner[:, pl.ds((blocks - 1 - j) * LANES, LANES)])
        at = pl.ds(j * LANES, LANES)
        tied[:, at] = 0.5 * (basis[:, at] + mirrored)
    both = tied[...]
    gram = 2.0 * dot(both, both, NT, HIGHEST)
    ratio[...] = loadings[...] / dot(gram, loadings[...], NN, HIGHEST)
    tied_high, tied_low = halves(both)
    tied_parts = jnp.concatenate([tied_high, tied_low], axis=0)
    for i in range(chunks):
        at = pl.ds(i * rows, rows)
        copies[i].wait()
        block_high, block_low = halves(stage[at, :])
        high[at, :] = block_high
        low[at, :] = block_low
        terms = dot(block_high, tied_parts, NT)
        terms = terms[:, :rank] + terms[:, rank:] + dot(block_low, tied_high, NT)
        numer[:, at] = terms.T


def terms_kernel(cols, own, other, ratio, high, low, new_loadings, keep, send):
    rank = own.shape[0]
    total = high.shape[1]
    half = total // 2
    new = ratio[...] * (own[...] + other[...])
    new_loadings[...] = new
    new_high, new_low = halves(new)
    new_parts = jnp.concatenate([new_high, new_low], axis=0)
    cross = dot(new, new, NT, HIGHEST)
    per_row = LANES // rank
    strip = rank // per_row
    packed = jnp.concatenate([cross[i * strip:(i + 1) * strip] for i in range(per_row)], axis=1)
    top = half // LANES * rank
    keep[pl.ds(top, strip), :] = packed
    send[pl.ds(top, strip), :] = jnp.zeros_like(packed)
    for c in range(0, total, cols):
        at = pl.ds(c, cols)
        terms = dot(new_parts, high[:, at], NN)
        terms = terms[:rank] + terms[rank:] + dot(new_high, low[:, at], NN)
        for b in range(cols // LANES):
            block = terms[:, b * LANES:(b + 1) * LANES]
            start = c + b * LANES
            if start < half:
                keep[pl.ds(start // LANES * rank, rank), :] = block
            else:
                turned = (total - LANES - start) // LANES * rank
                send[pl.ds(turned, rank), :] = mirror_lanes(block)


def basis_kernel(tied, own, other, new_basis):
    rank, cols = tied.shape
    half = cols // 2
    per_row = LANES // rank
    strip = rank // per_row
    top = half // LANES * rank
    packed = own[pl.ds(top, strip), :]
    cross = jnp.concatenate([packed[:, i * rank:(i + 1) * rank] for i in range(per_row)], axis=0)
    scale = dot(cross, tied[...], NN, HIGHEST)
    for start in range(0, cols, LANES):
        if start < half:
            numer = own[pl.ds(start // LANES * rank, rank), :]
        else:
            numer = mirror_lanes(other[pl.ds((cols - LANES - start) // LANES * rank, rank), :])
        at = pl.ds(start, LANES)
        new_basis[:, at] = tied[:, at] * (0.5 * numer) / scale[:, start:start + LANES]


def over_det(x):
    return lax.ppermute(x, "det", [(0, 1), (1, 0)])


def scan_sum(x):
    count = lax.axis_size("scan")
    steps = count.bit_length() - 1
    if count != 1 << steps:
        return lax.psum(x, "scan")
    for step in range(steps):
        route = []
        for core in range(2):
            stride = 1 << (step + core * (steps // 2)) % steps
            route += [(2 * i + core, 2 * (i ^ stride) + core) for i in range(count)]
        x = x + lax.ppermute(x, ("scan", "det"), route)
    return x


def per_device(spectra, basis, loadings):
    positions, cols = spectra.shape
    rank = basis.shape[0]
    rows = min(positions, 128)
    block_cols = 256
    packed = (cols // 2 // LANES * rank + rank * rank // LANES, LANES)
    partner = over_det(basis)
    numer, ratio, tied, high, low = pl.pallas_call(
        functools.partial(numer_kernel, rows),
        out_shape=[
            pltpu.VMEM((rank, positions), F32),
            pltpu.VMEM((rank, positions), F32),
            pltpu.VMEM((rank, cols), F32),
            pltpu.VMEM((positions, cols), BF16),
            pltpu.VMEM((positions, cols), BF16),
        ],
        in_specs=[pl.BlockSpec(memory_space=pl.ANY)] + vmem_specs(3),
        out_specs=vmem_specs(5),
        scratch_shapes=[pltpu.VMEM((positions, cols), F32), pltpu.SemaphoreType.DMA((positions // rows,))],
        compiler_params=pltpu.CompilerParams(vmem_limit_bytes=20 * MIB),
        name="numer",
    )(spectra, basis, partner, loadings)
    other = over_det(numer)
    new_loadings, keep, send = pl.pallas_call(
        functools.partial(terms_kernel, block_cols),
        out_shape=[
            jax.ShapeDtypeStruct((rank, positions), F32),
            pltpu.VMEM(packed, F32),
            pltpu.VMEM(packed, F32),
        ],
        in_specs=vmem_specs(5),
        out_specs=vmem_specs(3),
        compiler_params=pltpu.CompilerParams(vmem_limit_bytes=20 * MIB),
        name="terms",
    )(in_vmem(numer), in_vmem(other), in_vmem(ratio), in_vmem(high), in_vmem(low))
    sums = scan_sum(keep + over_det(send))
    new_basis = pl.pallas_call(
        basis_kernel,
        out_shape=jax.ShapeDtypeStruct((rank, cols), F32),
        in_specs=vmem_specs(3),
        out_specs=pl.BlockSpec(memory_space=pltpu.VMEM),
        compiler_params=pltpu.CompilerParams(vmem_limit_bytes=20 * MIB),
        name="basis",
    )(in_vmem(tied), in_vmem(sums), in_vmem(over_det(sums)))
    return new_loadings, new_basis


def solution(mesh):
    in_specs = (P(("grp", "scan"), "det"), P("grp", "det"), P("grp", "scan"))
    out_specs = (P("grp", "scan"), P("grp", "det"))
    return jax.shard_map(
        per_device, mesh=mesh, in_specs=in_specs, out_specs=out_specs, check_vma=False
    )
```

```python
import functools

import jax
import jax.numpy as jnp
from jax import lax
from jax.experimental import pallas as pl
from jax.experimental.pallas import tpu as pltpu
from jax.sharding import PartitionSpec as P

HIGHEST = lax.Precision.HIGHEST
LANES = 128
MIB = 1 << 20
F32, BF16 = jnp.float32, jnp.bfloat16
NT = (((1,), (1,)), ((), ()))
NN = (((1,), (0,)), ((), ()))
HBM, VMEM = pltpu.HBM, pltpu.VMEM


def call(kernel, name, ins, outs, scratch=(), flops=0, moved=0, aliases={}):
    params = pltpu.CompilerParams(vmem_limit_bytes=16 * MIB)
    return pl.pallas_call(
        kernel,
        out_shape=[memory(shape, dtype) for memory, shape, dtype in outs],
        in_specs=[pl.BlockSpec(memory_space=memory) for memory, _ in ins],
        out_specs=[pl.BlockSpec(memory_space=memory) for memory, _, _ in outs],
        scratch_shapes=list(scratch),
        input_output_aliases=aliases,
        compiler_params=params,
        cost_estimate=pl.CostEstimate(flops=flops, bytes_accessed=moved, transcendentals=0),
        name=name,
    )(*[pltpu.with_memory_space_constraint(x, memory) for memory, x in ins])


def halves(x):
    high = x.astype(BF16)
    return high, (x - high.astype(F32)).astype(BF16)


def both_halves(x):
    return jnp.concatenate(halves(x), axis=0)


def mirror_lanes(block):
    lane = lax.broadcasted_iota(jnp.int32, block.shape, 1)
    return jnp.take_along_axis(block, LANES - 1 - lane, axis=1, mode="promise_in_bounds")


def dot(a, b, dims, precision=None):
    return lax.dot_general(a, b, dims, precision=precision, preferred_element_type=F32)


def row_copies(spectra, stage, sems, first, rows):
    return [
        pltpu.make_async_copy(
            spectra.at[pl.ds(first + i * rows, rows)], stage.at[pl.ds(i * rows, rows)], sems.at[i]
        )
        for i in range(stage.shape[0] // rows)
    ]


def load_kernel(rows, spectra, basis, loadings, near_basis, near_loadings, high, low, stage, sems, side_sems):
    copies = row_copies(spectra, stage, sems, 0, rows)
    sides = [
        pltpu.make_async_copy(basis, near_basis, side_sems.at[0]),
        pltpu.make_async_copy(loadings, near_loadings, side_sems.at[1]),
    ]
    for copy in copies + sides:
        copy.start()
    for i, copy in enumerate(copies):
        at = pl.ds(i * rows, rows)
        copy.wait()
        high[at, :], low[at, :] = halves(stage[at, :])
    for copy in sides:
        copy.wait()


def numer_kernel(rows, spectra, basis, partner, high, low, numer, tied, late_high, late_low, stage, sems):
    rank, cols = basis.shape
    early = high.shape[0]
    copies = row_copies(spectra, stage, sems, early, rows)
    for copy in copies:
        copy.start()
    blocks = cols // LANES
    for j in range(blocks):
        mirrored = mirror_lanes(partner[:, pl.ds((blocks - 1 - j) * LANES, LANES)])
        at = pl.ds(j * LANES, LANES)
        tied[:, at] = 0.5 * (basis[:, at] + mirrored)
    tied_parts = both_halves(tied[...])

    def put(start, block_high, block_low):
        terms = dot(block_high, tied_parts, NT)
        terms = terms[:, :rank] + terms[:, rank:] + dot(block_low, tied_parts[:rank], NT)
        numer[:, pl.ds(start, block_high.shape[0])] = terms.T

    for start in range(0, early, rows):
        at = pl.ds(start, rows)
        put(start, high[at, :], low[at, :])
    for i, copy in enumerate(copies):
        at = pl.ds(i * rows, rows)
        copy.wait()
        block_high, block_low = halves(stage[at, :])
        late_high[at, :] = block_high
        late_low[at, :] = block_low
        put(early + i * rows, block_high, block_low)


def ratio_kernel(tied, loadings, ratio):
    gram = 2.0 * dot(tied[...], tied[...], NT, HIGHEST)
    ratio[...] = loadings[...] / dot(gram, loadings[...], NN, HIGHEST)


def column_terms(new, high, low, late_high, late_low, at):
    rank, early = new.shape[0], high.shape[0]
    parts = both_halves(new)
    terms = dot(parts[:, :early], high[:, at], NN) + dot(parts[:, early:], late_high[:, at], NN)
    rest = dot(parts[:rank, :early], low[:, at], NN) + dot(parts[:rank, early:], late_low[:, at], NN)
    return terms[:rank] + terms[rank:] + rest


def send_kernel(width, own, other, ratio, high, low, late_high, late_low, send):
    rank, cols = own.shape[0], high.shape[1]
    new = ratio[...] * (own[...] + other[...])
    for start in range(cols // 2, cols, width):
        terms = column_terms(new, high, low, late_high, late_low, pl.ds(start, width))
        for b in range(0, width, LANES):
            turned = (cols - LANES - start - b) // LANES * rank
            send[pl.ds(turned, rank), :] = mirror_lanes(terms[:, b:b + LANES])


def keep_kernel(width, own, other, ratio, high, low, late_high, late_low, new_loadings, keep, cross, new, sem):
    rank, cols = own.shape[0], high.shape[1]
    new[...] = ratio[...] * (own[...] + other[...])
    copy = pltpu.make_async_copy(new, new_loadings, sem)
    copy.start()
    for start in range(0, cols // 2, width):
        terms = column_terms(new[...], high, low, late_high, late_low, pl.ds(start, width))
        for b in range(0, width, LANES):
            keep[pl.ds((start + b) // LANES * rank, rank), :] = terms[:, b:b + LANES]
    square = dot(new[...], new[...], NT, HIGHEST)
    per_row = LANES // rank
    strip = rank // per_row
    cross[...] = jnp.concatenate([square[i * strip:(i + 1) * strip] for i in range(per_row)], axis=1)
    copy.wait()


def near_kernel(tied, sums, new_basis, scale, near, sem):
    rank, cols = tied.shape
    half = cols // 2
    per_row = LANES // rank
    strip = rank // per_row
    packed = sums[pl.ds(half // LANES * rank, strip), :]
    cross = jnp.concatenate([packed[:, i * rank:(i + 1) * rank] for i in range(per_row)], axis=0)
    whole = dot(cross, tied[...], NN, HIGHEST)
    scale[...] = whole[:, half:]
    for start in range(0, half, LANES):
        numer = sums[pl.ds(start // LANES * rank, rank), :]
        at = pl.ds(start, LANES)
        near[:, at] = tied[:, at] * (0.5 * numer) / whole[:, start:start + LANES]
    copy = pltpu.make_async_copy(near, new_basis.at[:, pl.ds(0, half)], sem)
    copy.start()
    copy.wait()


def far_kernel(first, tied, scale, sums, new_basis, far, sem):
    del first
    rank, cols = tied.shape
    half = cols // 2
    for start in range(0, half, LANES):
        numer = mirror_lanes(sums[pl.ds((half - LANES - start) // LANES * rank, rank), :])
        at = pl.ds(start, LANES)
        far[:, at] = tied[:, pl.ds(half + start, LANES)] * (0.5 * numer) / scale[:, at]
    copy = pltpu.make_async_copy(far, new_basis.at[:, pl.ds(half, half)], sem)
    copy.start()
    copy.wait()


def over_det(x):
    return lax.ppermute(x, "det", [(0, 1), (1, 0)])


def scan_sum(x):
    count = lax.axis_size("scan")
    steps = count.bit_length() - 1
    if count != 1 << steps:
        return lax.psum(x, "scan")
    for step in range(steps):
        route = []
        for core in range(2):
            stride = 1 << (step + core * (steps // 2)) % steps
            route += [(2 * i + core, 2 * (i ^ stride) + core) for i in range(count)]
        x = x + lax.ppermute(x, ("scan", "det"), route)
    return x


def per_device(spectra, basis, loadings):
    positions, cols = spectra.shape
    rank = basis.shape[0]
    half = cols // 2
    rows = 128
    early = positions // 2
    late = positions - early
    tall = half // LANES * rank
    strip = rank * rank // LANES
    product = 2 * rank * positions * cols
    dma = pltpu.SemaphoreType.DMA

    partner = over_det(basis)
    near_basis, near_loadings, high, low = call(
        functools.partial(load_kernel, rows), "load",
        [(HBM, spectra), (HBM, basis), (HBM, loadings)],
        [(VMEM, basis.shape, F32), (VMEM, loadings.shape, F32), (VMEM, (early, cols), BF16), (VMEM, (early, cols), BF16)],
        [VMEM((early, cols), F32), dma((early // rows,)), dma((2,))],
        moved=4 * early * cols,
    )
    numer, tied, late_high, late_low = call(
        functools.partial(numer_kernel, rows), "numer",
        [(HBM, spectra), (VMEM, near_basis), (VMEM, partner), (VMEM, high), (VMEM, low)],
        [(VMEM, loadings.shape, F32), (VMEM, basis.shape, F32), (VMEM, (late, cols), BF16), (VMEM, (late, cols), BF16)],
        [VMEM((late, cols), F32), dma((late // rows,))],
        flops=3 * product, moved=4 * late * cols,
    )
    other = over_det(numer)
    ratio, = call(ratio_kernel, "ratio", [(VMEM, tied), (VMEM, near_loadings)], [(VMEM, loadings.shape, F32)], flops=product // 16)
    operands = [(VMEM, x) for x in (numer, other, ratio, high, low, late_high, late_low)]
    send, = call(
        functools.partial(send_kernel, 256), "send", operands, [(VMEM, (tall, LANES), F32)], flops=3 * product // 2
    )
    received = over_det(send)
    new_loadings, keep, cross = call(
        functools.partial(keep_kernel, 256), "keep", operands,
        [(HBM, loadings.shape, F32), (VMEM, (tall, LANES), F32), (VMEM, (strip, LANES), F32)],
        [VMEM(loadings.shape, F32), dma(())],
        flops=3 * product // 2,
    )
    sums = scan_sum(jnp.concatenate([keep + received, cross], axis=0))
    others = over_det(sums)
    first, scale = call(
        near_kernel, "near", [(VMEM, tied), (VMEM, sums)],
        [(HBM, basis.shape, F32), (VMEM, (rank, half), F32)],
        [VMEM((rank, half), F32), dma(())],
        flops=product // 32,
    )
    new_basis, = call(
        far_kernel, "far", [(HBM, first), (VMEM, tied), (VMEM, scale), (VMEM, others)],
        [(HBM, basis.shape, F32)],
        [VMEM((rank, half), F32), dma(())],
        aliases={0: 0},
    )
    return new_loadings, new_basis


def solution(mesh):
    in_specs = (P(("grp", "scan"), "det"), P("grp", "det"), P("grp", "scan"))
    out_specs = (P("grp", "scan"), P("grp", "det"))
    return jax.shard_map(
        per_device, mesh=mesh, in_specs=in_specs, out_specs=out_specs, check_vma=False
    )
```

```python
import functools

import jax
import jax.numpy as jnp
from jax import lax
from jax.experimental import pallas as pl
from jax.experimental.pallas import tpu as pltpu
from jax.sharding import PartitionSpec as P

HIGHEST = lax.Precision.HIGHEST
LANES = 128
MIB = 1 << 20
F32, BF16 = jnp.float32, jnp.bfloat16
NT = (((1,), (1,)), ((), ()))
NN = (((1,), (0,)), ((), ()))
HBM, VMEM = pltpu.HBM, pltpu.VMEM


def call(kernel, name, ins, outs, scratch=(), flops=0, moved=0):
    params = pltpu.CompilerParams(vmem_limit_bytes=16 * MIB)
    return pl.pallas_call(
        kernel,
        out_shape=[memory(shape, dtype) for memory, shape, dtype in outs],
        in_specs=[pl.BlockSpec(memory_space=memory) for memory, _ in ins],
        out_specs=[pl.BlockSpec(memory_space=memory) for memory, _, _ in outs],
        scratch_shapes=list(scratch),
        compiler_params=params,
        cost_estimate=pl.CostEstimate(flops=flops, bytes_accessed=moved, transcendentals=0),
        name=name,
    )(*[pltpu.with_memory_space_constraint(x, memory) for memory, x in ins])


def halves(x):
    high = x.astype(BF16)
    return high, (x - high.astype(F32)).astype(BF16)


def both_halves(x):
    return jnp.concatenate(halves(x), axis=0)


def mirror_lanes(block):
    lane = lax.broadcasted_iota(jnp.int32, block.shape, 1)
    return jnp.take_along_axis(block, LANES - 1 - lane, axis=1, mode="promise_in_bounds")


def dot(a, b, dims, precision=None):
    return lax.dot_general(a, b, dims, precision=precision, preferred_element_type=F32)


def row_copies(spectra, stage, sems, first, rows):
    return [
        pltpu.make_async_copy(
            spectra.at[pl.ds(first + i * rows, rows)], stage.at[pl.ds(i * rows, rows)], sems.at[i]
        )
        for i in range(stage.shape[0] // rows)
    ]


def load_kernel(rows, spectra, basis, loadings, near_basis, near_loadings, high, low, stage, sems, side_sems):
    copies = row_copies(spectra, stage, sems, 0, rows)
    sides = [
        pltpu.make_async_copy(basis, near_basis, side_sems.at[0]),
        pltpu.make_async_copy(loadings, near_loadings, side_sems.at[1]),
    ]
    for copy in copies + sides:
        copy.start()
    for i, copy in enumerate(copies):
        at = pl.ds(i * rows, rows)
        copy.wait()
        high[at, :], low[at, :] = halves(stage[at, :])
    for copy in sides:
        copy.wait()


def numer_kernel(rows, spectra, basis, partner, high, low, numer, tied, late_high, late_low, stage, sems):
    rank, cols = basis.shape
    early = high.shape[0]
    copies = row_copies(spectra, stage, sems, early, rows)
    for copy in copies:
        copy.start()
    blocks = cols // LANES
    for j in range(blocks):
        mirrored = mirror_lanes(partner[:, pl.ds((blocks - 1 - j) * LANES, LANES)])
        at = pl.ds(j * LANES, LANES)
        tied[:, at] = 0.5 * (basis[:, at] + mirrored)
    tied_parts = both_halves(tied[...])

    def put(start, block_high, block_low):
        terms = dot(block_high, tied_parts, NT)
        terms = terms[:, :rank] + terms[:, rank:] + dot(block_low, tied_parts[:rank], NT)
        numer[:, pl.ds(start, block_high.shape[0])] = terms.T

    for start in range(0, early, rows):
        at = pl.ds(start, rows)
        put(start, high[at, :], low[at, :])
    for i, copy in enumerate(copies):
        at = pl.ds(i * rows, rows)
        copy.wait()
        block_high, block_low = halves(stage[at, :])
        late_high[at, :] = block_high
        late_low[at, :] = block_low
        put(early + i * rows, block_high, block_low)


def ratio_kernel(tied, loadings, ratio):
    gram = 2.0 * dot(tied[...], tied[...], NT, HIGHEST)
    ratio[...] = loadings[...] / dot(gram, loadings[...], NN, HIGHEST)


def column_terms(new, high, low, late_high, late_low, at):
    rank, early = new.shape[0], high.shape[0]
    parts = both_halves(new)
    terms = dot(parts[:, :early], high[:, at], NN) + dot(parts[:, early:], late_high[:, at], NN)
    rest = dot(parts[:rank, :early], low[:, at], NN) + dot(parts[:rank, early:], late_low[:, at], NN)
    return terms[:rank] + terms[rank:] + rest


def odd_chip():
    count = lax.axis_size("scan")
    index = lax.axis_index("scan")
    ones = sum(index // (1 << bit) % 2 for bit in range(scan_steps()))
    return ones % 2 if count == 1 << scan_steps() else index * 0


def scan_steps():
    return lax.axis_size("scan").bit_length() - 1


def place(block, blocks, turned):
    return block + turned * (blocks - 1 - 2 * block)


def maybe_mirror(block, turned):
    lane = lax.broadcasted_iota(jnp.int32, block.shape, 1)
    return jnp.take_along_axis(block, place(lane, LANES, turned), axis=1, mode="promise_in_bounds")


def half_terms(width, new, arrays, turned, first, out):
    rank, cols = new.shape[0], arrays[0].shape[1]
    half, last = cols // 2, first + out.shape[0] // rank
    wide = width // LANES
    for block in range(first, last, wide):
        group = min(wide, last - block)
        start = block * LANES + turned * (half + (half // LANES - 2 * block - group) * LANES)
        terms = column_terms(new, *arrays, pl.ds(pl.multiple_of(start, LANES), group * LANES))
        for b in range(group):
            row = (block - first + place(b, group, turned)) * rank
            part = maybe_mirror(terms[:, b * LANES:(b + 1) * LANES], turned)
            out[pl.ds(pl.multiple_of(row, rank), rank), :] = part


def send_kernel(width, own, other, ratio, high, low, late_high, late_low, send):
    new = ratio[...] * (own[...] + other[...])
    half_terms(width, new, (high, low, late_high, late_low), 1 - odd_chip(), 0, send)


def keep_kernel(width, own, other, ratio, high, low, late_high, late_low, new_loadings, keep, cross, new, sem):
    rank = own.shape[0]
    new[...] = ratio[...] * (own[...] + other[...])
    copy = pltpu.make_async_copy(new, new_loadings, sem)
    copy.start()
    half_terms(width, new[...], (high, low, late_high, late_low), odd_chip(), 0, keep)
    square = dot(new[...], new[...], NT, HIGHEST)
    per_row = LANES // rank
    strip = rank // per_row
    cross[...] = jnp.concatenate([square[i * strip:(i + 1) * strip] for i in range(per_row)], axis=1)
    copy.wait()


def half_basis(tied, scale, numers, turned, out):
    rank, cols = tied.shape
    half = cols // 2
    for block in range(half // LANES):
        numer = maybe_mirror(numers[block * rank:(block + 1) * rank], turned)
        column = place(block, half // LANES, turned) * LANES
        at = pl.ds(pl.multiple_of(turned * half + column, LANES), LANES)
        out[:, pl.ds(pl.multiple_of(column, LANES), LANES)] = tied[:, at] * (0.5 * numer) / scale[:, at]


def near_kernel(tied, sums, more, scale, near):
    rank = tied.shape[0]
    per_row = LANES // rank
    strip = rank // per_row
    packed = sums[:strip, :]
    cross = jnp.concatenate([packed[:, i * rank:(i + 1) * rank] for i in range(per_row)], axis=0)
    scale[...] = dot(cross, tied[...], NN, HIGHEST)
    numers = jnp.concatenate([sums[strip:, :], more[...]], axis=0)
    half_basis(tied, scale, numers, odd_chip(), near)


def far_kernel(tied, scale, near, sums, more, new_basis, far, sems):
    half = near.shape[1]
    odd = odd_chip()
    copies = [
        pltpu.make_async_copy(
            part, new_basis.at[:, pl.ds(pl.multiple_of(turned * half, LANES), half)], sems.at[i]
        )
        for i, (part, turned) in enumerate(((near, odd), (far, 1 - odd)))
    ]
    copies[0].start()
    numers = jnp.concatenate([sums[...], more[...]], axis=0)
    half_basis(tied, scale, numers, 1 - odd, far)
    copies[1].start()
    for copy in copies:
        copy.wait()


def over_det(x):
    return lax.ppermute(x, "det", [(0, 1), (1, 0)])


def stride_orders(steps):
    cuts = [round(steps * i / 3) for i in range(4)]
    groups = [list(range(a, b)) for a, b in zip(cuts, cuts[1:])]
    return [
        [sum((groups[g] for g in order), []) for order in stream]
        for stream in (((1, 0, 2), (0, 2, 1)), ((1, 2, 0), (2, 1, 0)))
    ]


def scan_sums(parts):
    count, steps = lax.axis_size("scan"), scan_steps()
    if count != 1 << steps:
        return lax.psum(parts, "scan")
    orders = stride_orders(steps)
    for step in range(steps):
        received = []
        for part, order in zip(parts, orders):
            route = []
            for i in range(count):
                for core in range(2):
                    half = (core + i.bit_count()) % 2
                    route.append((2 * i + core, 2 * (i ^ 1 << order[half][step]) + 1 - core))
            received.append(lax.ppermute(part, ("scan", "det"), route))
        parts = [part + other for part, other in zip(parts, received)]
    return parts


def per_device(spectra, basis, loadings):
    positions, cols = spectra.shape
    rank = basis.shape[0]
    half = cols // 2
    rows = 128
    early = positions // 2
    late = positions - early
    tall = half // LANES * rank
    strip = rank * rank // LANES
    product = 2 * rank * positions * cols
    dma = pltpu.SemaphoreType.DMA

    partner = over_det(basis)
    near_basis, near_loadings, high, low = call(
        functools.partial(load_kernel, rows), "load",
        [(HBM, spectra), (HBM, basis), (HBM, loadings)],
        [(VMEM, basis.shape, F32), (VMEM, loadings.shape, F32), (VMEM, (early, cols), BF16), (VMEM, (early, cols), BF16)],
        [VMEM((early, cols), F32), dma((early // rows,)), dma((2,))],
        moved=4 * early * cols,
    )
    numer, tied, late_high, late_low = call(
        functools.partial(numer_kernel, 2 * rows), "numer",
        [(HBM, spectra), (VMEM, near_basis), (VMEM, partner), (VMEM, high), (VMEM, low)],
        [(VMEM, loadings.shape, F32), (VMEM, basis.shape, F32), (VMEM, (late, cols), BF16), (VMEM, (late, cols), BF16)],
        [VMEM((late, cols), F32), dma((late // (2 * rows),))],
        flops=3 * product, moved=4 * late * cols,
    )
    other = over_det(numer)
    ratio, = call(ratio_kernel, "ratio", [(VMEM, tied), (VMEM, near_loadings)], [(VMEM, loadings.shape, F32)], flops=product // 16)
    operands = [(VMEM, x) for x in (numer, other, ratio, high, low, late_high, late_low)]
    send, = call(
        functools.partial(send_kernel, 256), "send", operands, [(VMEM, (tall, LANES), F32)], flops=3 * product // 2
    )
    received = over_det(send)
    new_loadings, keep, cross = call(
        functools.partial(keep_kernel, 256), "keep", operands,
        [(HBM, loadings.shape, F32), (VMEM, (tall, LANES), F32), (VMEM, (strip, LANES), F32)],
        [VMEM(loadings.shape, F32), dma(())],
        flops=3 * product // 2,
    )
    folded = keep + received
    cut = tall // 2
    parts = (jnp.concatenate([cross, folded[:cut]], axis=0), folded[cut:])
    sums = scan_sums(lax.optimization_barrier(parts))
    others = [over_det(sums[0][strip:]), over_det(sums[1])]
    scale, near = call(
        near_kernel, "near", [(VMEM, tied), (VMEM, sums[0]), (VMEM, sums[1])],
        [(VMEM, basis.shape, F32), (VMEM, (rank, half), F32)],
        flops=product // 32,
    )
    new_basis, = call(
        far_kernel, "far", [(VMEM, x) for x in (tied, scale, near, *others)],
        [(HBM, basis.shape, F32)],
        [VMEM((rank, half), F32), dma((2,))],
    )
    return new_loadings, new_basis


def solution(mesh):
    in_specs = (P(("grp", "scan"), "det"), P("grp", "det"), P("grp", "scan"))
    out_specs = (P("grp", "scan"), P("grp", "det"))
    return jax.shard_map(
        per_device, mesh=mesh, in_specs=in_specs, out_specs=out_specs, check_vma=False
    )
```

```python
import functools

import jax
import jax.numpy as jnp
from jax import lax
from jax.experimental import pallas as pl
from jax.experimental.pallas import tpu as pltpu
from jax.sharding import PartitionSpec as P

HIGHEST = lax.Precision.HIGHEST
LANES = 128
MIB = 1 << 20
F32, BF16 = jnp.float32, jnp.bfloat16
NT = (((1,), (1,)), ((), ()))
NN = (((1,), (0,)), ((), ()))
HBM, VMEM = pltpu.HBM, pltpu.VMEM


def call(kernel, name, ins, outs, scratch=(), flops=0, moved=0):
    params = pltpu.CompilerParams(vmem_limit_bytes=16 * MIB)
    return pl.pallas_call(
        kernel,
        out_shape=[memory(shape, dtype) for memory, shape, dtype in outs],
        in_specs=[pl.BlockSpec(memory_space=memory) for memory, _ in ins],
        out_specs=[pl.BlockSpec(memory_space=memory) for memory, _, _ in outs],
        scratch_shapes=list(scratch),
        compiler_params=params,
        cost_estimate=pl.CostEstimate(flops=flops, bytes_accessed=moved, transcendentals=0),
        name=name,
    )(*[pltpu.with_memory_space_constraint(x, memory) for memory, x in ins])


def halves(x):
    high = x.astype(BF16)
    return high, (x - high.astype(F32)).astype(BF16)


def both_halves(x):
    return jnp.concatenate(halves(x), axis=0)


def mirror_lanes(block):
    lane = lax.broadcasted_iota(jnp.int32, block.shape, 1)
    return jnp.take_along_axis(block, LANES - 1 - lane, axis=1, mode="promise_in_bounds")


def dot(a, b, dims, precision=None):
    return lax.dot_general(a, b, dims, precision=precision, preferred_element_type=F32)


def row_copies(spectra, stage, sems, first, rows):
    return [
        pltpu.make_async_copy(
            spectra.at[pl.ds(first + i * rows, rows)], stage.at[pl.ds(i * rows, rows)], sems.at[i]
        )
        for i in range(stage.shape[0] // rows)
    ]


def load_kernel(rows, spectra, basis, loadings, near_basis, near_loadings, high, low, stage, sems, side_sems):
    copies = row_copies(spectra, stage, sems, 0, rows)
    sides = [
        pltpu.make_async_copy(basis, near_basis, side_sems.at[0]),
        pltpu.make_async_copy(loadings, near_loadings, side_sems.at[1]),
    ]
    for copy in copies + sides:
        copy.start()
    for i, copy in enumerate(copies):
        at = pl.ds(i * rows, rows)
        copy.wait()
        high[at, :], low[at, :] = halves(stage[at, :])
    for copy in sides:
        copy.wait()


def numer_kernel(rows, spectra, basis, partner, high, low, numer, tied, late_high, late_low, stage, sems):
    rank, cols = basis.shape
    early = high.shape[0]
    copies = row_copies(spectra, stage, sems, early, rows)
    for copy in copies:
        copy.start()
    blocks = cols // LANES
    for j in range(blocks):
        mirrored = mirror_lanes(partner[:, pl.ds((blocks - 1 - j) * LANES, LANES)])
        at = pl.ds(j * LANES, LANES)
        tied[:, at] = 0.5 * (basis[:, at] + mirrored)
    tied_parts = both_halves(tied[...])

    def put(start, block_high, block_low):
        terms = dot(block_high, tied_parts, NT)
        terms = terms[:, :rank] + terms[:, rank:] + dot(block_low, tied_parts[:rank], NT)
        numer[:, pl.ds(start, block_high.shape[0])] = terms.T

    for start in range(0, early, rows):
        at = pl.ds(start, rows)
        put(start, high[at, :], low[at, :])
    for i, copy in enumerate(copies):
        at = pl.ds(i * rows, rows)
        copy.wait()
        block_high, block_low = halves(stage[at, :])
        late_high[at, :] = block_high
        late_low[at, :] = block_low
        put(early + i * rows, block_high, block_low)


def ratio_kernel(tied, loadings, ratio):
    gram = 2.0 * dot(tied[...], tied[...], NT, HIGHEST)
    ratio[...] = loadings[...] / dot(gram, loadings[...], NN, HIGHEST)


def column_terms(new, high, low, late_high, late_low, at):
    rank, early = new.shape[0], high.shape[0]
    parts = both_halves(new)
    terms = dot(parts[:, :early], high[:, at], NN) + dot(parts[:, early:], late_high[:, at], NN)
    rest = dot(parts[:rank, :early], low[:, at], NN) + dot(parts[:rank, early:], late_low[:, at], NN)
    return terms[:rank] + terms[rank:] + rest


def odd_chip():
    count = lax.axis_size("scan")
    index = lax.axis_index("scan")
    ones = sum(index // (1 << bit) % 2 for bit in range(scan_steps()))
    return ones % 2 if count == 1 << scan_steps() else index * 0


def scan_steps():
    return lax.axis_size("scan").bit_length() - 1


def place(block, blocks, turned):
    return block + turned * (blocks - 1 - 2 * block)


def maybe_mirror(block, turned):
    lane = lax.broadcasted_iota(jnp.int32, block.shape, 1)
    return jnp.take_along_axis(block, place(lane, LANES, turned), axis=1, mode="promise_in_bounds")


def half_terms(width, new, arrays, turned, first, out):
    rank, cols = new.shape[0], arrays[0].shape[1]
    half, last = cols // 2, first + out.shape[0] // rank
    wide = width // LANES
    for block in range(first, last, wide):
        group = min(wide, last - block)
        start = block * LANES + turned * (half + (half // LANES - 2 * block - group) * LANES)
        terms = column_terms(new, *arrays, pl.ds(pl.multiple_of(start, LANES), group * LANES))
        for b in range(group):
            row = (block - first + place(b, group, turned)) * rank
            part = maybe_mirror(terms[:, b * LANES:(b + 1) * LANES], turned)
            out[pl.ds(pl.multiple_of(row, rank), rank), :] = part


def send_kernel(width, own, other, ratio, high, low, late_high, late_low, send):
    new = ratio[...] * (own[...] + other[...])
    half_terms(width, new, (high, low, late_high, late_low), 1 - odd_chip(), 0, send)


def keep_kernel(width, own, other, ratio, high, low, late_high, late_low, new_loadings, keep, cross, stage, sem):
    rank = own.shape[0]
    new = ratio[...] * (own[...] + other[...])
    stage[...] = new
    copy = pltpu.make_async_copy(stage, new_loadings, sem)
    copy.start()
    square = dot(new, new, NT, HIGHEST)
    per_row = LANES // rank
    strip = rank // per_row
    cross[...] = jnp.concatenate([square[i * strip:(i + 1) * strip] for i in range(per_row)], axis=1)
    half_terms(width, new, (high, low, late_high, late_low), odd_chip(), 0, keep)
    copy.wait()


def piece_start(turned, first, count, blocks):
    return pl.multiple_of((first + turned * (2 * blocks - 2 * first - count)) * LANES, LANES)


def basis_piece(tied, scale, numers, turned, first, out):
    rank, cols = tied.shape
    count = numers.shape[0] // rank
    start = piece_start(turned, first, count, cols // 2 // LANES)
    for block in range(count):
        numer = maybe_mirror(numers[block * rank:(block + 1) * rank], turned)
        column = pl.multiple_of(place(block, count, turned) * LANES, LANES)
        at = pl.ds(pl.multiple_of(start + column, LANES), LANES)
        out[:, pl.ds(column, LANES)] = tied[:, at] * (0.5 * numer) / scale[:, at]


def first_kernel(tied, sums, scale, near):
    rank = tied.shape[0]
    per_row = LANES // rank
    strip = rank // per_row
    packed = sums[:strip, :]
    cross = jnp.concatenate([packed[:, i * rank:(i + 1) * rank] for i in range(per_row)], axis=0)
    scale[...] = dot(cross, tied[...], NN, HIGHEST)
    basis_piece(tied, scale, sums[strip:, :], odd_chip(), 0, near)


def middle_kernel(first, tied, scale, sums, others, near, far):
    odd = odd_chip()
    basis_piece(tied, scale, sums[...], odd, first, near)
    basis_piece(tied, scale, others[...], 1 - odd, 0, far)


def last_kernel(first, tied, scale, near, more, far, others, new_basis, rest, sems):
    cols = tied.shape[1]
    blocks = cols // 2 // LANES
    odd = odd_chip()
    copies = []
    for i, (piece, turned, begin) in enumerate(
        ((near, odd, 0), (more, odd, first), (far, 1 - odd, 0), (rest, 1 - odd, first))
    ):
        if piece is rest:
            basis_piece(tied, scale, others[...], turned, first, rest)
        width = piece.shape[1]
        start = piece_start(turned, begin, width // LANES, blocks)
        copies.append(pltpu.make_async_copy(piece, new_basis.at[:, pl.ds(start, width)], sems.at[i]))
        copies[-1].start()
    for copy in copies:
        copy.wait()


def over_det(x):
    return lax.ppermute(x, "det", [(0, 1), (1, 0)])


def stride_orders(steps):
    cuts = [round(steps * i / 3) for i in range(4)]
    groups = [list(range(a, b)) for a, b in zip(cuts, cuts[1:])]
    return [
        [sum((groups[g] for g in order), []) for order in stream]
        for stream in (((1, 0, 2), (2, 1, 0)), ((1, 2, 0), (2, 0, 1)))
    ]


def scan_sums(parts):
    count, steps = lax.axis_size("scan"), scan_steps()
    if count != 1 << steps:
        return [(total, jnp.zeros_like(total)) for total in lax.psum(parts, "scan")]
    orders = stride_orders(steps)
    pairs = [(part, jnp.zeros_like(part)) for part in parts]
    for step in range(steps):
        received = []
        for part, order in zip(parts, orders):
            route = []
            for i in range(count):
                for core in range(2):
                    half = (core + i.bit_count()) % 2
                    route.append((2 * i + core, 2 * (i ^ 1 << order[half][step]) + 1 - core))
            received.append(lax.ppermute(part, ("scan", "det"), route))
        pairs = list(zip(parts, received))
        parts = [part + other for part, other in pairs]
    return pairs


def per_device(spectra, basis, loadings):
    positions, cols = spectra.shape
    rank = basis.shape[0]
    half = cols // 2
    rows = 128
    early = positions // 2
    late = positions - early
    tall = half // LANES * rank
    strip = rank * rank // LANES
    product = 2 * rank * positions * cols
    dma = pltpu.SemaphoreType.DMA

    partner = over_det(basis)
    near_basis, near_loadings, high, low = call(
        functools.partial(load_kernel, rows), "load",
        [(HBM, spectra), (HBM, basis), (HBM, loadings)],
        [(VMEM, basis.shape, F32), (VMEM, loadings.shape, F32), (VMEM, (early, cols), BF16), (VMEM, (early, cols), BF16)],
        [VMEM((early, cols), F32), dma((early // rows,)), dma((2,))],
        moved=4 * early * cols,
    )
    numer, tied, late_high, late_low = call(
        functools.partial(numer_kernel, 2 * rows), "numer",
        [(HBM, spectra), (VMEM, near_basis), (VMEM, partner), (VMEM, high), (VMEM, low)],
        [(VMEM, loadings.shape, F32), (VMEM, basis.shape, F32), (VMEM, (late, cols), BF16), (VMEM, (late, cols), BF16)],
        [VMEM((late, cols), F32), dma((late // (2 * rows),))],
        flops=3 * product, moved=4 * late * cols,
    )
    other = over_det(numer)
    ratio, = call(ratio_kernel, "ratio", [(VMEM, tied), (VMEM, near_loadings)], [(VMEM, loadings.shape, F32)], flops=product // 16)
    operands = [(VMEM, x) for x in (numer, other, ratio, high, low, late_high, late_low)]
    send, = call(
        functools.partial(send_kernel, 512), "send", operands, [(VMEM, (tall, LANES), F32)], flops=3 * product // 2
    )
    received = over_det(send)
    new_loadings, keep, cross = call(
        functools.partial(keep_kernel, 512), "keep", operands,
        [(HBM, loadings.shape, F32), (VMEM, (tall, LANES), F32), (VMEM, (strip, LANES), F32)],
        [VMEM(loadings.shape, F32), dma(())],
        flops=3 * product // 2,
    )
    folded = keep + received
    cut = tall // rank // 2 * rank
    parts = (jnp.concatenate([cross, folded[:cut]], axis=0), folded[cut:])
    (mine, theirs), (my_rest, their_rest) = scan_sums(lax.optimization_barrier(parts))
    sums = mine + theirs
    others = over_det(sums[strip:])
    scale, near = call(
        first_kernel, "first", [(VMEM, tied), (VMEM, sums)],
        [(VMEM, basis.shape, F32), (VMEM, (rank, cut // rank * LANES), F32)],
        flops=product // 32,
    )
    scale, near, their_rest = lax.optimization_barrier((scale, near, their_rest))
    rest = my_rest + their_rest
    other_rest = over_det(rest)
    wide = (rank, half - cut // rank * LANES)
    more, far = call(
        functools.partial(middle_kernel, cut // rank), "middle",
        [(VMEM, x) for x in (tied, scale, rest, others)],
        [(VMEM, wide, F32), (VMEM, near.shape, F32)],
        flops=product // 64,
    )
    new_basis, = call(
        functools.partial(last_kernel, cut // rank), "last",
        [(VMEM, x) for x in (tied, scale, near, more, far, other_rest)],
        [(HBM, basis.shape, F32)],
        [VMEM(wide, F32), dma((4,))],
    )
    return new_loadings, new_basis


def solution(mesh):
    in_specs = (P(("grp", "scan"), "det"), P("grp", "det"), P("grp", "scan"))
    out_specs = (P("grp", "scan"), P("grp", "det"))
    return jax.shard_map(
        per_device, mesh=mesh, in_specs=in_specs, out_specs=out_specs, check_vma=False
    )
```

```python
import functools

import jax
import jax.numpy as jnp
from jax import lax
from jax.experimental import pallas as pl
from jax.experimental.pallas import tpu as pltpu
from jax.sharding import PartitionSpec as P

HIGHEST = lax.Precision.HIGHEST
LANES = 128
MIB = 1 << 20
F32, BF16 = jnp.float32, jnp.bfloat16
NT = (((1,), (1,)), ((), ()))
NN = (((1,), (0,)), ((), ()))
HBM, VMEM = pltpu.HBM, pltpu.VMEM


def call(kernel, name, ins, outs, scratch=(), flops=0, moved=0):
    params = pltpu.CompilerParams(vmem_limit_bytes=16 * MIB)
    return pl.pallas_call(
        kernel,
        out_shape=[memory(shape, dtype) for memory, shape, dtype in outs],
        in_specs=[pl.BlockSpec(memory_space=memory) for memory, _ in ins],
        out_specs=[pl.BlockSpec(memory_space=memory) for memory, _, _ in outs],
        scratch_shapes=list(scratch),
        compiler_params=params,
        cost_estimate=pl.CostEstimate(flops=flops, bytes_accessed=moved, transcendentals=0),
        name=name,
    )(*[pltpu.with_memory_space_constraint(x, memory) for memory, x in ins])


def halves(x):
    high = x.astype(BF16)
    return high, (x - high.astype(F32)).astype(BF16)


def both_halves(x):
    return jnp.concatenate(halves(x), axis=0)


def mirror_lanes(block):
    lane = lax.broadcasted_iota(jnp.int32, block.shape, 1)
    return jnp.take_along_axis(block, LANES - 1 - lane, axis=1, mode="promise_in_bounds")


def dot(a, b, dims, precision=None):
    return lax.dot_general(a, b, dims, precision=precision, preferred_element_type=F32)


def row_copies(spectra, stage, sems, first, sizes):
    copies, start = [], 0
    for i, rows in enumerate(sizes):
        at = pl.ds(start, rows)
        copies.append((at, pltpu.make_async_copy(spectra.at[pl.ds(first + start, rows)], stage.at[at], sems.at[i])))
        start += rows
    return copies


def load_kernel(sizes, spectra, basis, loadings, near_basis, near_loadings, high, low, stage, sems, side_sems):
    copies = row_copies(spectra, stage, sems, 0, sizes)
    sides = [
        pltpu.make_async_copy(basis, near_basis, side_sems.at[0]),
        pltpu.make_async_copy(loadings, near_loadings, side_sems.at[1]),
    ]
    for copy in [copy for _, copy in copies] + sides:
        copy.start()
    for at, copy in copies:
        copy.wait()
        high[at, :], low[at, :] = halves(stage[at, :])
    for copy in sides:
        copy.wait()


def numer_kernel(group, sizes, spectra, basis, partner, high, low, numer, tied, late_high, late_low, stage, sems):
    rank, cols = basis.shape
    early = high.shape[0]
    copies = row_copies(spectra, stage, sems, early, sizes)
    for _, copy in copies:
        copy.start()
    blocks = cols // LANES
    for j in range(blocks):
        mirrored = mirror_lanes(partner[:, pl.ds((blocks - 1 - j) * LANES, LANES)])
        at = pl.ds(j * LANES, LANES)
        tied[:, at] = 0.5 * (basis[:, at] + mirrored)
    tied_parts = both_halves(tied[...])

    def put(start, block_high, block_low):
        terms = dot(block_high, tied_parts, NT)
        terms = terms[:, :rank] + terms[:, rank:] + dot(block_low, tied_parts[:rank], NT)
        numer[:, pl.ds(start, block_high.shape[0])] = terms.T

    for start in range(0, early, group):
        at = pl.ds(start, min(group, early - start))
        put(start, high[at, :], low[at, :])
    for whole, copy in copies:
        copy.wait()
        late_high[whole, :], late_low[whole, :] = halves(stage[whole, :])
        put(early + whole.start, late_high[whole, :], late_low[whole, :])


def ratio_kernel(tied, loadings, ratio):
    gram = 2.0 * dot(tied[...], tied[...], NT, HIGHEST)
    ratio[...] = loadings[...] / dot(gram, loadings[...], NN, HIGHEST)


def column_terms(new, high, low, late_high, late_low, at):
    rank, early = new.shape[0], high.shape[0]
    parts = both_halves(new)
    terms = dot(parts[:, :early], high[:, at], NN) + dot(parts[:, early:], late_high[:, at], NN)
    rest = dot(parts[:rank, :early], low[:, at], NN) + dot(parts[:rank, early:], late_low[:, at], NN)
    return terms[:rank] + terms[rank:] + rest


def odd_chip():
    count = lax.axis_size("scan")
    index = lax.axis_index("scan")
    ones = sum(index // (1 << bit) % 2 for bit in range(scan_steps()))
    return ones % 2 if count == 1 << scan_steps() else index * 0


def scan_steps():
    return lax.axis_size("scan").bit_length() - 1


def place(block, blocks, turned):
    return block + turned * (blocks - 1 - 2 * block)


def maybe_mirror(block, turned):
    lane = lax.broadcasted_iota(jnp.int32, block.shape, 1)
    return jnp.take_along_axis(block, place(lane, LANES, turned), axis=1, mode="promise_in_bounds")


def half_terms(width, new, arrays, turned, first, out):
    rank, cols = new.shape[0], arrays[0].shape[1]
    half, last = cols // 2, first + out.shape[0] // rank
    wide = width // LANES
    for block in range(first, last, wide):
        group = min(wide, last - block)
        start = block * LANES + turned * (half + (half // LANES - 2 * block - group) * LANES)
        terms = column_terms(new, *arrays, pl.ds(pl.multiple_of(start, LANES), group * LANES))
        for b in range(group):
            row = (block - first + place(b, group, turned)) * rank
            part = maybe_mirror(terms[:, b * LANES:(b + 1) * LANES], turned)
            out[pl.ds(pl.multiple_of(row, rank), rank), :] = part


def send_kernel(width, own, other, ratio, high, low, late_high, late_low, send):
    new = ratio[...] * (own[...] + other[...])
    half_terms(width, new, (high, low, late_high, late_low), 1 - odd_chip(), 0, send)


def keep_kernel(width, own, other, ratio, high, low, late_high, late_low, new_loadings, keep, cross, stage, sem):
    rank = own.shape[0]
    new = ratio[...] * (own[...] + other[...])
    stage[...] = new
    copy = pltpu.make_async_copy(stage, new_loadings, sem)
    copy.start()
    square = dot(new, new, NT, HIGHEST)
    per_row = LANES // rank
    strip = rank // per_row
    cross[...] = jnp.concatenate([square[i * strip:(i + 1) * strip] for i in range(per_row)], axis=1)
    half_terms(width, new, (high, low, late_high, late_low), odd_chip(), 0, keep)
    copy.wait()


def piece_start(turned, first, count, blocks):
    return pl.multiple_of((first + turned * (2 * blocks - 2 * first - count)) * LANES, LANES)


def basis_piece(tied, scale, numers, turned, first, out):
    rank, cols = tied.shape
    count = numers.shape[0] // rank
    start = piece_start(turned, first, count, cols // 2 // LANES)
    for block in range(count):
        numer = maybe_mirror(numers[block * rank:(block + 1) * rank], turned)
        column = pl.multiple_of(place(block, count, turned) * LANES, LANES)
        at = pl.ds(pl.multiple_of(start + column, LANES), LANES)
        out[:, pl.ds(column, LANES)] = tied[:, at] * (0.5 * numer) / scale[:, at]


def first_kernel(tied, sums, scale, near):
    rank = tied.shape[0]
    per_row = LANES // rank
    strip = rank // per_row
    packed = sums[:strip, :]
    cross = jnp.concatenate([packed[:, i * rank:(i + 1) * rank] for i in range(per_row)], axis=0)
    scale[...] = dot(cross, tied[...], NN, HIGHEST)
    basis_piece(tied, scale, sums[strip:, :], odd_chip(), 0, near)


def middle_kernel(first, tied, scale, sums, others, near, far):
    odd = odd_chip()
    basis_piece(tied, scale, sums[...], odd, first, near)
    basis_piece(tied, scale, others[...], 1 - odd, 0, far)


def last_kernel(first, tied, scale, near, more, far, others, new_basis, rest, sems):
    cols = tied.shape[1]
    blocks = cols // 2 // LANES
    odd = odd_chip()
    copies = []
    for i, (piece, turned, begin) in enumerate(
        ((near, odd, 0), (more, odd, first), (far, 1 - odd, 0), (rest, 1 - odd, first))
    ):
        if piece is rest:
            basis_piece(tied, scale, others[...], turned, first, rest)
        width = piece.shape[1]
        start = piece_start(turned, begin, width // LANES, blocks)
        copies.append(pltpu.make_async_copy(piece, new_basis.at[:, pl.ds(start, width)], sems.at[i]))
        copies[-1].start()
    for copy in copies:
        copy.wait()


def over_det(x):
    return lax.ppermute(x, "det", [(0, 1), (1, 0)])


def stride_orders(steps):
    cuts = [round(steps * i / 3) for i in range(4)]
    groups = [list(range(a, b)) for a, b in zip(cuts, cuts[1:])]
    return [
        [sum((groups[g] for g in order), []) for order in stream]
        for stream in (((1, 0, 2), (2, 1, 0)), ((1, 2, 0), (2, 0, 1)))
    ]


def scan_sums(parts):
    count, steps = lax.axis_size("scan"), scan_steps()
    if count != 1 << steps:
        return [(total, jnp.zeros_like(total)) for total in lax.psum(parts, "scan")]
    orders = stride_orders(steps)
    pairs = [(part, jnp.zeros_like(part)) for part in parts]
    for step in range(steps):
        received = []
        for part, order in zip(parts, orders):
            route = []
            for i in range(count):
                for core in range(2):
                    half = (core + i.bit_count()) % 2
                    route.append((2 * i + core, 2 * (i ^ 1 << order[half][step]) + 1 - core))
            received.append(lax.ppermute(part, ("scan", "det"), route))
        pairs = list(zip(parts, received))
        parts = [part + other for part, other in pairs]
    return pairs


def per_device(spectra, basis, loadings):
    positions, cols = spectra.shape
    rank = basis.shape[0]
    half = cols // 2
    early = positions // 2
    late = positions - early
    early_sizes = (early // 2, early // 4, early // 8, early // 8)
    late_sizes = (late // 2, late // 2)
    tall = half // LANES * rank
    strip = rank * rank // LANES
    product = 2 * rank * positions * cols
    dma = pltpu.SemaphoreType.DMA

    partner = over_det(basis)
    near_basis, near_loadings, high, low = call(
        functools.partial(load_kernel, early_sizes), "load",
        [(HBM, spectra), (HBM, basis), (HBM, loadings)],
        [(VMEM, basis.shape, F32), (VMEM, loadings.shape, F32), (VMEM, (early, cols), BF16), (VMEM, (early, cols), BF16)],
        [VMEM((early, cols), F32), dma((len(early_sizes),)), dma((2,))],
        moved=4 * early * cols,
    )
    numer, tied, late_high, late_low = call(
        functools.partial(numer_kernel, 128, late_sizes), "numer",
        [(HBM, spectra), (VMEM, near_basis), (VMEM, partner), (VMEM, high), (VMEM, low)],
        [(VMEM, loadings.shape, F32), (VMEM, basis.shape, F32), (VMEM, (late, cols), BF16), (VMEM, (late, cols), BF16)],
        [VMEM((late, cols), F32), dma((len(late_sizes),))],
        flops=3 * product, moved=4 * late * cols,
    )
    other = over_det(numer)
    ratio, = call(ratio_kernel, "ratio", [(VMEM, tied), (VMEM, near_loadings)], [(VMEM, loadings.shape, F32)], flops=product // 16)
    operands = [(VMEM, x) for x in (numer, other, ratio, high, low, late_high, late_low)]
    send, = call(
        functools.partial(send_kernel, 512), "send", operands, [(VMEM, (tall, LANES), F32)], flops=3 * product // 2
    )
    received = over_det(send)
    new_loadings, keep, cross = call(
        functools.partial(keep_kernel, 512), "keep", operands,
        [(HBM, loadings.shape, F32), (VMEM, (tall, LANES), F32), (VMEM, (strip, LANES), F32)],
        [VMEM(loadings.shape, F32), dma(())],
        flops=3 * product // 2,
    )
    folded = keep + received
    cut = tall // rank // 2 * rank
    parts = (jnp.concatenate([cross, folded[:cut]], axis=0), folded[cut:])
    (mine, theirs), (my_rest, their_rest) = scan_sums(lax.optimization_barrier(parts))
    sums = mine + theirs
    others = over_det(sums[strip:])
    scale, near = call(
        first_kernel, "first", [(VMEM, tied), (VMEM, sums)],
        [(VMEM, basis.shape, F32), (VMEM, (rank, cut // rank * LANES), F32)],
        flops=product // 32,
    )
    scale, near, their_rest = lax.optimization_barrier((scale, near, their_rest))
    rest = my_rest + their_rest
    other_rest = over_det(rest)
    wide = (rank, half - cut // rank * LANES)
    more, far = call(
        functools.partial(middle_kernel, cut // rank), "middle",
        [(VMEM, x) for x in (tied, scale, rest, others)],
        [(VMEM, wide, F32), (VMEM, near.shape, F32)],
        flops=product // 64,
    )
    new_basis, = call(
        functools.partial(last_kernel, cut // rank), "last",
        [(VMEM, x) for x in (tied, scale, near, more, far, other_rest)],
        [(HBM, basis.shape, F32)],
        [VMEM(wide, F32), dma((4,))],
    )
    return new_loadings, new_basis


def solution(mesh):
    in_specs = (P(("grp", "scan"), "det"), P("grp", "det"), P("grp", "scan"))
    out_specs = (P("grp", "scan"), P("grp", "det"))
    return jax.shard_map(
        per_device, mesh=mesh, in_specs=in_specs, out_specs=out_specs, check_vma=False
    )
```

```python
import functools

import jax
import jax.numpy as jnp
from jax import lax
from jax.experimental import pallas as pl
from jax.experimental.pallas import tpu as pltpu
from jax.sharding import PartitionSpec as P

HIGHEST = lax.Precision.HIGHEST
LANES = 128
MIB = 1 << 20
F32, BF16 = jnp.float32, jnp.bfloat16
NT = (((1,), (1,)), ((), ()))
NN = (((1,), (0,)), ((), ()))
HBM, VMEM = pltpu.HBM, pltpu.VMEM


def call(kernel, name, ins, outs, scratch=(), flops=0, moved=0, aliases=None):
    params = pltpu.CompilerParams(vmem_limit_bytes=16 * MIB)
    return pl.pallas_call(
        kernel,
        out_shape=[memory(shape, dtype) for memory, shape, dtype in outs],
        in_specs=[pl.BlockSpec(memory_space=memory) for memory, _ in ins],
        out_specs=[pl.BlockSpec(memory_space=memory) for memory, _, _ in outs],
        scratch_shapes=list(scratch),
        input_output_aliases=aliases or {},
        compiler_params=params,
        cost_estimate=pl.CostEstimate(flops=flops, bytes_accessed=moved, transcendentals=0),
        name=name,
    )(*[pltpu.with_memory_space_constraint(x, memory) for memory, x in ins])


def halves(x):
    high = x.astype(BF16)
    return high, (x - high.astype(F32)).astype(BF16)


def both_halves(x):
    return jnp.concatenate(halves(x), axis=0)


def mirror_lanes(block):
    lane = lax.broadcasted_iota(jnp.int32, block.shape, 1)
    return jnp.take_along_axis(block, LANES - 1 - lane, axis=1, mode="promise_in_bounds")


def dot(a, b, dims, precision=None):
    return lax.dot_general(a, b, dims, precision=precision, preferred_element_type=F32)


def row_copies(spectra, stage, sems, first, sizes):
    copies, start = [], 0
    for i, rows in enumerate(sizes):
        at = pl.ds(start, rows)
        copies.append((at, pltpu.make_async_copy(spectra.at[pl.ds(first + start, rows)], stage.at[at], sems.at[i])))
        start += rows
    return copies


def load_kernel(sizes, spectra, basis, loadings, near_basis, near_loadings, high, low, stage, sems, side_sems):
    copies = row_copies(spectra, stage, sems, 0, sizes)
    sides = [
        pltpu.make_async_copy(basis, near_basis, side_sems.at[0]),
        pltpu.make_async_copy(loadings, near_loadings, side_sems.at[1]),
    ]
    for copy in [copy for _, copy in copies] + sides:
        copy.start()
    for at, copy in copies:
        copy.wait()
        high[at, :], low[at, :] = halves(stage[at, :])
    for copy in sides:
        copy.wait()


def numer_kernel(group, sizes, spectra, basis, partner, high, low, numer, tied, late_high, late_low, stage, sems):
    rank, cols = basis.shape
    early = high.shape[0]
    copies = row_copies(spectra, stage, sems, early, sizes)
    for _, copy in copies:
        copy.start()
    blocks = cols // LANES
    for j in range(blocks):
        mirrored = mirror_lanes(partner[:, pl.ds((blocks - 1 - j) * LANES, LANES)])
        at = pl.ds(j * LANES, LANES)
        tied[:, at] = 0.5 * (basis[:, at] + mirrored)
    tied_parts = both_halves(tied[...])

    def put(start, block_high, block_low):
        terms = dot(block_high, tied_parts, NT)
        terms = terms[:, :rank] + terms[:, rank:] + dot(block_low, tied_parts[:rank], NT)
        numer[:, pl.ds(start, block_high.shape[0])] = terms.T

    for start in range(0, early, group):
        at = pl.ds(start, min(group, early - start))
        put(start, high[at, :], low[at, :])
    for whole, copy in copies:
        copy.wait()
        late_high[whole, :], late_low[whole, :] = halves(stage[whole, :])
        put(early + whole.start, late_high[whole, :], late_low[whole, :])


def ratio_kernel(tied, loadings, ratio):
    gram = 2.0 * dot(tied[...], tied[...], NT, HIGHEST)
    ratio[...] = loadings[...] / dot(gram, loadings[...], NN, HIGHEST)


def column_terms(new, high, low, late_high, late_low, at):
    rank, early = new.shape[0], high.shape[0]
    parts = both_halves(new)
    terms = dot(parts[:, :early], high[:, at], NN) + dot(parts[:, early:], late_high[:, at], NN)
    rest = dot(parts[:rank, :early], low[:, at], NN) + dot(parts[:rank, early:], late_low[:, at], NN)
    return terms[:rank] + terms[rank:] + rest


def odd_chip():
    count = lax.axis_size("scan")
    index = lax.axis_index("scan")
    ones = sum(index // (1 << bit) % 2 for bit in range(scan_steps()))
    return ones % 2 if count == 1 << scan_steps() else index * 0


def scan_steps():
    return lax.axis_size("scan").bit_length() - 1


def place(block, blocks, turned):
    return block + turned * (blocks - 1 - 2 * block)


def maybe_mirror(block, turned):
    lane = lax.broadcasted_iota(jnp.int32, block.shape, 1)
    return jnp.take_along_axis(block, place(lane, LANES, turned), axis=1, mode="promise_in_bounds")


def half_terms(width, new, arrays, turned, first, out):
    rank, cols = new.shape[0], arrays[0].shape[1]
    half, last = cols // 2, first + out.shape[0] // rank
    wide = width // LANES
    for block in range(first, last, wide):
        group = min(wide, last - block)
        start = block * LANES + turned * (half + (half // LANES - 2 * block - group) * LANES)
        terms = column_terms(new, *arrays, pl.ds(pl.multiple_of(start, LANES), group * LANES))
        for b in range(group):
            row = (block - first + place(b, group, turned)) * rank
            part = maybe_mirror(terms[:, b * LANES:(b + 1) * LANES], turned)
            out[pl.ds(pl.multiple_of(row, rank), rank), :] = part


def send_kernel(width, own, other, ratio, high, low, late_high, late_low, send):
    new = ratio[...] * (own[...] + other[...])
    half_terms(width, new, (high, low, late_high, late_low), 1 - odd_chip(), 0, send)


def keep_kernel(width, own, other, ratio, high, low, late_high, late_low, new_loadings, keep, cross, stage, sem):
    rank = own.shape[0]
    new = ratio[...] * (own[...] + other[...])
    stage[...] = new
    copy = pltpu.make_async_copy(stage, new_loadings, sem)
    copy.start()
    square = dot(new, new, NT, HIGHEST)
    per_row = LANES // rank
    strip = rank // per_row
    cross[...] = jnp.concatenate([square[i * strip:(i + 1) * strip] for i in range(per_row)], axis=1)
    half_terms(width, new, (high, low, late_high, late_low), odd_chip(), 0, keep)
    copy.wait()


def piece_start(turned, first, count, blocks):
    return pl.multiple_of((first + turned * (2 * blocks - 2 * first - count)) * LANES, LANES)


def basis_piece(tied, scale, numers, turned, first, out):
    rank, cols = tied.shape
    count = numers.shape[0] // rank
    start = piece_start(turned, first, count, cols // 2 // LANES)
    for block in range(count):
        numer = maybe_mirror(numers[block * rank:(block + 1) * rank], turned)
        column = pl.multiple_of(place(block, count, turned) * LANES, LANES)
        at = pl.ds(pl.multiple_of(start + column, LANES), LANES)
        out[:, pl.ds(column, LANES)] = tied[:, at] * (0.5 * numer) / scale[:, at]


def first_kernel(tied, sums, scale, near):
    rank = tied.shape[0]
    per_row = LANES // rank
    strip = rank // per_row
    packed = sums[:strip, :]
    cross = jnp.concatenate([packed[:, i * rank:(i + 1) * rank] for i in range(per_row)], axis=0)
    scale[...] = dot(cross, tied[...], NN, HIGHEST)
    basis_piece(tied, scale, sums[strip:, :], odd_chip(), 0, near)


def write_pieces(new_basis, pieces, sems):
    blocks = new_basis.shape[1] // 2 // LANES
    copies = []
    for i, (piece, turned, first) in enumerate(pieces):
        width = piece.shape[1]
        start = piece_start(turned, first, width // LANES, blocks)
        copies.append(pltpu.make_async_copy(piece, new_basis.at[:, pl.ds(start, width)], sems.at[i]))
        copies[-1].start()
    return copies


def middle_kernel(first, tied, scale, near, sums, others, new_basis, more, far, sems):
    odd = odd_chip()
    basis_piece(tied, scale, sums[...], odd, first, more)
    basis_piece(tied, scale, others[...], 1 - odd, 0, far)
    for copy in write_pieces(new_basis, ((near, odd, 0), (more, odd, first), (far, 1 - odd, 0)), sems):
        copy.wait()


def last_kernel(first, begun, tied, scale, others, new_basis, rest, sems):
    del begun
    turned = 1 - odd_chip()
    basis_piece(tied, scale, others[...], turned, first, rest)
    for copy in write_pieces(new_basis, ((rest, turned, first),), sems):
        copy.wait()


def over_det(x):
    return lax.ppermute(x, "det", [(0, 1), (1, 0)])


def stride_orders(steps):
    cuts = [round(steps * i / 3) for i in range(4)]
    groups = [list(range(a, b)) for a, b in zip(cuts, cuts[1:])]
    return [
        [sum((groups[g] for g in order), []) for order in stream]
        for stream in (((1, 0, 2), (2, 1, 0)), ((1, 2, 0), (2, 0, 1)))
    ]


def scan_sums(parts):
    count, steps = lax.axis_size("scan"), scan_steps()
    if count != 1 << steps:
        return [(total, jnp.zeros_like(total)) for total in lax.psum(parts, "scan")]
    orders = stride_orders(steps)
    pairs = [(part, jnp.zeros_like(part)) for part in parts]
    for step in range(steps):
        received = []
        for part, order in zip(parts, orders):
            route = []
            for i in range(count):
                for core in range(2):
                    half = (core + i.bit_count()) % 2
                    route.append((2 * i + core, 2 * (i ^ 1 << order[half][step]) + 1 - core))
            received.append(lax.ppermute(part, ("scan", "det"), route))
        pairs = list(zip(parts, received))
        parts = [part + other for part, other in pairs]
    return pairs


def per_device(spectra, basis, loadings):
    positions, cols = spectra.shape
    rank = basis.shape[0]
    half = cols // 2
    early = positions // 2
    late = positions - early
    early_sizes = (early // 2, early // 4, early // 8, early // 8)
    late_sizes = (late // 2, late // 2)
    tall = half // LANES * rank
    strip = rank * rank // LANES
    product = 2 * rank * positions * cols
    dma = pltpu.SemaphoreType.DMA

    partner = over_det(basis)
    near_basis, near_loadings, high, low = call(
        functools.partial(load_kernel, early_sizes), "load",
        [(HBM, spectra), (HBM, basis), (HBM, loadings)],
        [(VMEM, basis.shape, F32), (VMEM, loadings.shape, F32), (VMEM, (early, cols), BF16), (VMEM, (early, cols), BF16)],
        [VMEM((early, cols), F32), dma((len(early_sizes),)), dma((2,))],
        moved=4 * early * cols,
    )
    numer, tied, late_high, late_low = call(
        functools.partial(numer_kernel, 128, late_sizes), "numer",
        [(HBM, spectra), (VMEM, near_basis), (VMEM, partner), (VMEM, high), (VMEM, low)],
        [(VMEM, loadings.shape, F32), (VMEM, basis.shape, F32), (VMEM, (late, cols), BF16), (VMEM, (late, cols), BF16)],
        [VMEM((late, cols), F32), dma((len(late_sizes),))],
        flops=3 * product, moved=4 * late * cols,
    )
    other = over_det(numer)
    ratio, = call(ratio_kernel, "ratio", [(VMEM, tied), (VMEM, near_loadings)], [(VMEM, loadings.shape, F32)], flops=product // 16)
    operands = [(VMEM, x) for x in (numer, other, ratio, high, low, late_high, late_low)]
    send, = call(
        functools.partial(send_kernel, 512), "send", operands, [(VMEM, (tall, LANES), F32)], flops=3 * product // 2
    )
    received = over_det(send)
    new_loadings, keep, cross = call(
        functools.partial(keep_kernel, 512), "keep", operands,
        [(HBM, loadings.shape, F32), (VMEM, (tall, LANES), F32), (VMEM, (strip, LANES), F32)],
        [VMEM(loadings.shape, F32), dma(())],
        flops=3 * product // 2,
    )
    folded = keep + received
    cut = tall // rank // 2 * rank
    parts = (jnp.concatenate([cross, folded[:cut]], axis=0), folded[cut:])
    (mine, theirs), (my_rest, their_rest) = scan_sums(lax.optimization_barrier(parts))
    sums = mine + theirs
    others = over_det(sums[strip:])
    scale, near = call(
        first_kernel, "first", [(VMEM, tied), (VMEM, sums)],
        [(VMEM, basis.shape, F32), (VMEM, (rank, cut // rank * LANES), F32)],
        flops=product // 32,
    )
    scale, near, their_rest = lax.optimization_barrier((scale, near, their_rest))
    rest = my_rest + their_rest
    other_rest = over_det(rest)
    wide = (rank, half - cut // rank * LANES)
    begun, = call(
        functools.partial(middle_kernel, cut // rank), "middle",
        [(VMEM, x) for x in (tied, scale, near, rest, others)],
        [(HBM, basis.shape, F32)],
        [VMEM(wide, F32), VMEM(near.shape, F32), dma((3,))],
        flops=product // 64,
    )
    new_basis, = call(
        functools.partial(last_kernel, cut // rank), "last",
        [(HBM, begun)] + [(VMEM, x) for x in (tied, scale, other_rest)],
        [(HBM, basis.shape, F32)],
        [VMEM(wide, F32), dma((1,))],
        aliases={0: 0},
    )
    return new_loadings, new_basis


def solution(mesh):
    in_specs = (P(("grp", "scan"), "det"), P("grp", "det"), P("grp", "scan"))
    out_specs = (P("grp", "scan"), P("grp", "det"))
    return jax.shard_map(
        per_device, mesh=mesh, in_specs=in_specs, out_specs=out_specs, check_vma=False
    )
```

```python
import functools

import jax
import jax.numpy as jnp
from jax import lax
from jax.experimental import pallas as pl
from jax.experimental.pallas import tpu as pltpu
from jax.sharding import PartitionSpec as P

HIGHEST = lax.Precision.HIGHEST
LANES = 128
MIB = 1 << 20
F32, BF16 = jnp.float32, jnp.bfloat16
NT = (((1,), (1,)), ((), ()))
NN = (((1,), (0,)), ((), ()))
HBM, VMEM = pltpu.HBM, pltpu.VMEM


def call(kernel, name, ins, outs, scratch=(), flops=0, moved=0):
    params = pltpu.CompilerParams(vmem_limit_bytes=16 * MIB)
    return pl.pallas_call(
        kernel,
        out_shape=[memory(shape, dtype) for memory, shape, dtype in outs],
        in_specs=[pl.BlockSpec(memory_space=memory) for memory, _ in ins],
        out_specs=[pl.BlockSpec(memory_space=memory) for memory, _, _ in outs],
        scratch_shapes=list(scratch),
        compiler_params=params,
        cost_estimate=pl.CostEstimate(flops=flops, bytes_accessed=moved, transcendentals=0),
        name=name,
    )(*[pltpu.with_memory_space_constraint(x, memory) for memory, x in ins])


def halves(x):
    high = x.astype(BF16)
    return high, (x - high.astype(F32)).astype(BF16)


def both_halves(x):
    return jnp.concatenate(halves(x), axis=0)


def mirror_lanes(block):
    lane = lax.broadcasted_iota(jnp.int32, block.shape, 1)
    return jnp.take_along_axis(block, LANES - 1 - lane, axis=1, mode="promise_in_bounds")


def dot(a, b, dims, precision=None):
    return lax.dot_general(a, b, dims, precision=precision, preferred_element_type=F32)


def row_copies(spectra, stage, sems, first, sizes):
    copies, start = [], 0
    for i, rows in enumerate(sizes):
        at = pl.ds(start, rows)
        copies.append((at, pltpu.make_async_copy(spectra.at[pl.ds(first + start, rows)], stage.at[at], sems.at[i])))
        start += rows
    return copies


def load_kernel(sizes, spectra, basis, loadings, near_basis, near_loadings, high, low, stage, sems, side_sems):
    copies = row_copies(spectra, stage, sems, 0, sizes)
    sides = [
        pltpu.make_async_copy(basis, near_basis, side_sems.at[0]),
        pltpu.make_async_copy(loadings, near_loadings, side_sems.at[1]),
    ]
    for copy in [copy for _, copy in copies] + sides:
        copy.start()
    for at, copy in copies:
        copy.wait()
        high[at, :], low[at, :] = halves(stage[at, :])
    for copy in sides:
        copy.wait()


def numer_kernel(group, sizes, spectra, basis, partner, high, low, numer, tied, late_high, late_low, stage, sems):
    rank, cols = basis.shape
    early = high.shape[0]
    copies = row_copies(spectra, stage, sems, early, sizes)
    for _, copy in copies:
        copy.start()
    blocks = cols // LANES
    for j in range(blocks):
        mirrored = mirror_lanes(partner[:, pl.ds((blocks - 1 - j) * LANES, LANES)])
        at = pl.ds(j * LANES, LANES)
        tied[:, at] = 0.5 * (basis[:, at] + mirrored)
    tied_parts = both_halves(tied[...])

    def put(start, block_high, block_low):
        terms = dot(block_high, tied_parts, NT)
        terms = terms[:, :rank] + terms[:, rank:] + dot(block_low, tied_parts[:rank], NT)
        numer[:, pl.ds(start, block_high.shape[0])] = terms.T

    def turn(start, block_high, block_low):
        terms = dot(tied_parts, block_high, NT)
        numer[:, pl.ds(start, block_high.shape[0])] = (
            terms[:rank] + terms[rank:] + dot(tied_parts[:rank], block_low, NT)
        )

    for start in range(0, early, group):
        at = pl.ds(start, min(group, early - start))
        (turn if start // group % 2 == 1 else put)(start, high[at, :], low[at, :])
    for whole, copy in copies:
        copy.wait()
        late_high[whole, :], late_low[whole, :] = halves(stage[whole, :])
        size = whole.size // 2
        for i, step in enumerate((put, turn)):
            at = pl.ds(whole.start + i * size, size)
            step(early + at.start, late_high[at, :], late_low[at, :])


def ratio_kernel(tied, loadings, ratio):
    gram = 2.0 * dot(tied[...], tied[...], NT, HIGHEST)
    ratio[...] = loadings[...] / dot(gram, loadings[...], NN, HIGHEST)


def column_terms(new, high, low, late_high, late_low, at):
    rank, early = new.shape[0], high.shape[0]
    parts = both_halves(new)
    terms = dot(parts[:, :early], high[:, at], NN) + dot(parts[:, early:], late_high[:, at], NN)
    rest = dot(parts[:rank, :early], low[:, at], NN) + dot(parts[:rank, early:], late_low[:, at], NN)
    return terms[:rank] + terms[rank:] + rest


def odd_chip():
    count = lax.axis_size("scan")
    index = lax.axis_index("scan")
    ones = sum(index // (1 << bit) % 2 for bit in range(scan_steps()))
    return ones % 2 if count == 1 << scan_steps() else index * 0


def scan_steps():
    return lax.axis_size("scan").bit_length() - 1


def place(block, blocks, turned):
    return block + turned * (blocks - 1 - 2 * block)


def maybe_mirror(block, turned):
    lane = lax.broadcasted_iota(jnp.int32, block.shape, 1)
    return jnp.take_along_axis(block, place(lane, LANES, turned), axis=1, mode="promise_in_bounds")


def half_terms(width, new, arrays, turned, first, out):
    rank, cols = new.shape[0], arrays[0].shape[1]
    half, last = cols // 2, first + out.shape[0] // rank
    wide = width // LANES
    for block in range(first, last, wide):
        group = min(wide, last - block)
        start = block * LANES + turned * (half + (half // LANES - 2 * block - group) * LANES)
        terms = column_terms(new, *arrays, pl.ds(pl.multiple_of(start, LANES), group * LANES))
        for b in range(group):
            row = (block - first + place(b, group, turned)) * rank
            part = maybe_mirror(terms[:, b * LANES:(b + 1) * LANES], turned)
            out[pl.ds(pl.multiple_of(row, rank), rank), :] = part


def send_kernel(width, own, other, ratio, high, low, late_high, late_low, send):
    new = ratio[...] * (own[...] + other[...])
    half_terms(width, new, (high, low, late_high, late_low), 1 - odd_chip(), 0, send)


def keep_kernel(width, own, other, ratio, high, low, late_high, late_low, new_loadings, keep, cross, stage, sem):
    rank = own.shape[0]
    new = ratio[...] * (own[...] + other[...])
    stage[...] = new
    copy = pltpu.make_async_copy(stage, new_loadings, sem)
    copy.start()
    square = dot(new, new, NT, HIGHEST)
    per_row = LANES // rank
    strip = rank // per_row
    cross[...] = jnp.concatenate([square[i * strip:(i + 1) * strip] for i in range(per_row)], axis=1)
    half_terms(width, new, (high, low, late_high, late_low), odd_chip(), 0, keep)
    copy.wait()


def piece_start(turned, first, count, blocks):
    return pl.multiple_of((first + turned * (2 * blocks - 2 * first - count)) * LANES, LANES)


def basis_piece(tied, scale, numers, turned, first, out):
    rank, cols = tied.shape
    count = numers.shape[0] // rank
    start = piece_start(turned, first, count, cols // 2 // LANES)
    for block in range(count):
        numer = maybe_mirror(numers[block * rank:(block + 1) * rank], turned)
        column = pl.multiple_of(place(block, count, turned) * LANES, LANES)
        at = pl.ds(pl.multiple_of(start + column, LANES), LANES)
        out[:, pl.ds(column, LANES)] = tied[:, at] * (0.5 * numer) / scale[:, at]


def first_kernel(tied, sums, scale, near):
    rank = tied.shape[0]
    per_row = LANES // rank
    strip = rank // per_row
    packed = sums[:strip, :]
    cross = jnp.concatenate([packed[:, i * rank:(i + 1) * rank] for i in range(per_row)], axis=0)
    scale[...] = dot(cross, tied[...], NN, HIGHEST)
    basis_piece(tied, scale, sums[strip:, :], odd_chip(), 0, near)


def middle_kernel(first, tied, scale, sums, others, near, far):
    odd = odd_chip()
    basis_piece(tied, scale, sums[...], odd, first, near)
    basis_piece(tied, scale, others[...], 1 - odd, 0, far)


def last_kernel(first, tied, scale, near, more, far, others, new_basis, rest, sems):
    cols = tied.shape[1]
    blocks = cols // 2 // LANES
    odd = odd_chip()
    copies = []
    for i, (piece, turned, begin) in enumerate(
        ((near, odd, 0), (more, odd, first), (far, 1 - odd, 0), (rest, 1 - odd, first))
    ):
        if piece is rest:
            basis_piece(tied, scale, others[...], turned, first, rest)
        width = piece.shape[1]
        start = piece_start(turned, begin, width // LANES, blocks)
        copies.append(pltpu.make_async_copy(piece, new_basis.at[:, pl.ds(start, width)], sems.at[i]))
        copies[-1].start()
    for copy in copies:
        copy.wait()


def over_det(x):
    return lax.ppermute(x, "det", [(0, 1), (1, 0)])


def stride_orders(steps):
    cuts = [round(steps * i / 3) for i in range(4)]
    groups = [list(range(a, b)) for a, b in zip(cuts, cuts[1:])]
    return [
        [sum((groups[g] for g in order), []) for order in stream]
        for stream in (((1, 0, 2), (2, 1, 0)), ((1, 2, 0), (2, 0, 1)))
    ]


def scan_sums(parts):
    count, steps = lax.axis_size("scan"), scan_steps()
    if count != 1 << steps:
        return [(total, jnp.zeros_like(total)) for total in lax.psum(parts, "scan")]
    orders = stride_orders(steps)
    pairs = [(part, jnp.zeros_like(part)) for part in parts]
    for step in range(steps):
        received = []
        for part, order in zip(parts, orders):
            route = []
            for i in range(count):
                for core in range(2):
                    half = (core + i.bit_count()) % 2
                    route.append((2 * i + core, 2 * (i ^ 1 << order[half][step]) + 1 - core))
            received.append(lax.ppermute(part, ("scan", "det"), route))
        pairs = list(zip(parts, received))
        parts = [part + other for part, other in pairs]
    return pairs


def per_device(spectra, basis, loadings):
    positions, cols = spectra.shape
    rank = basis.shape[0]
    half = cols // 2
    early = positions // 2
    late = positions - early
    early_sizes = (early // 2, early // 4, early // 8, early // 8)
    late_sizes = (late // 2, late // 2)
    tall = half // LANES * rank
    strip = rank * rank // LANES
    product = 2 * rank * positions * cols
    dma = pltpu.SemaphoreType.DMA

    partner = over_det(basis)
    near_basis, near_loadings, high, low = call(
        functools.partial(load_kernel, early_sizes), "load",
        [(HBM, spectra), (HBM, basis), (HBM, loadings)],
        [(VMEM, basis.shape, F32), (VMEM, loadings.shape, F32), (VMEM, (early, cols), BF16), (VMEM, (early, cols), BF16)],
        [VMEM((early, cols), F32), dma((len(early_sizes),)), dma((2,))],
        moved=4 * early * cols,
    )
    numer, tied, late_high, late_low = call(
        functools.partial(numer_kernel, 128, late_sizes), "numer",
        [(HBM, spectra), (VMEM, near_basis), (VMEM, partner), (VMEM, high), (VMEM, low)],
        [(VMEM, loadings.shape, F32), (VMEM, basis.shape, F32), (VMEM, (late, cols), BF16), (VMEM, (late, cols), BF16)],
        [VMEM((late, cols), F32), dma((len(late_sizes),))],
        flops=3 * product, moved=4 * late * cols,
    )
    other = over_det(numer)
    ratio, = call(ratio_kernel, "ratio", [(VMEM, tied), (VMEM, near_loadings)], [(VMEM, loadings.shape, F32)], flops=product // 16)
    operands = [(VMEM, x) for x in (numer, other, ratio, high, low, late_high, late_low)]
    send, = call(
        functools.partial(send_kernel, 512), "send", operands, [(VMEM, (tall, LANES), F32)], flops=3 * product // 2
    )
    received = over_det(send)
    new_loadings, keep, cross = call(
        functools.partial(keep_kernel, 512), "keep", operands,
        [(HBM, loadings.shape, F32), (VMEM, (tall, LANES), F32), (VMEM, (strip, LANES), F32)],
        [VMEM(loadings.shape, F32), dma(())],
        flops=3 * product // 2,
    )
    folded = keep + received
    cut = tall // rank // 2 * rank
    parts = (jnp.concatenate([cross, folded[:cut]], axis=0), folded[cut:])
    (mine, theirs), (my_rest, their_rest) = scan_sums(lax.optimization_barrier(parts))
    sums = mine + theirs
    others = over_det(sums[strip:])
    scale, near = call(
        first_kernel, "first", [(VMEM, tied), (VMEM, sums)],
        [(VMEM, basis.shape, F32), (VMEM, (rank, cut // rank * LANES), F32)],
        flops=product // 32,
    )
    scale, near, their_rest = lax.optimization_barrier((scale, near, their_rest))
    rest = my_rest + their_rest
    other_rest = over_det(rest)
    wide = (rank, half - cut // rank * LANES)
    more, far = call(
        functools.partial(middle_kernel, cut // rank), "middle",
        [(VMEM, x) for x in (tied, scale, rest, others)],
        [(VMEM, wide, F32), (VMEM, near.shape, F32)],
        flops=product // 64,
    )
    new_basis, = call(
        functools.partial(last_kernel, cut // rank), "last",
        [(VMEM, x) for x in (tied, scale, near, more, far, other_rest)],
        [(HBM, basis.shape, F32)],
        [VMEM(wide, F32), dma((4,))],
    )
    return new_loadings, new_basis


def solution(mesh):
    in_specs = (P(("grp", "scan"), "det"), P("grp", "det"), P("grp", "scan"))
    out_specs = (P("grp", "scan"), P("grp", "det"))
    return jax.shard_map(
        per_device, mesh=mesh, in_specs=in_specs, out_specs=out_specs, check_vma=False
    )
```

```python
import functools

import jax
import jax.numpy as jnp
from jax import lax
from jax.experimental import pallas as pl
from jax.experimental.pallas import tpu as pltpu
from jax.sharding import PartitionSpec as P

HIGHEST = lax.Precision.HIGHEST
LANES = 128
MIB = 1 << 20
F32, BF16 = jnp.float32, jnp.bfloat16
NT = (((1,), (1,)), ((), ()))
NN = (((1,), (0,)), ((), ()))
HBM, VMEM = pltpu.HBM, pltpu.VMEM


def call(kernel, name, ins, outs, scratch=(), flops=0, moved=0):
    params = pltpu.CompilerParams(vmem_limit_bytes=16 * MIB)
    return pl.pallas_call(
        kernel,
        out_shape=[memory(shape, dtype) for memory, shape, dtype in outs],
        in_specs=[pl.BlockSpec(memory_space=memory) for memory, _ in ins],
        out_specs=[pl.BlockSpec(memory_space=memory) for memory, _, _ in outs],
        scratch_shapes=list(scratch),
        compiler_params=params,
        cost_estimate=pl.CostEstimate(flops=flops, bytes_accessed=moved, transcendentals=0),
        name=name,
    )(*[pltpu.with_memory_space_constraint(x, memory) for memory, x in ins])


def halves(x):
    high = x.astype(BF16)
    return high, (x - high.astype(F32)).astype(BF16)


def both_halves(x):
    return jnp.concatenate(halves(x), axis=0)


def mirror_lanes(block):
    lane = lax.broadcasted_iota(jnp.int32, block.shape, 1)
    return jnp.take_along_axis(block, LANES - 1 - lane, axis=1, mode="promise_in_bounds")


def dot(a, b, dims, precision=None):
    return lax.dot_general(a, b, dims, precision=precision, preferred_element_type=F32)


def row_copies(spectra, stage, sems, first, sizes):
    copies, start = [], 0
    for i, rows in enumerate(sizes):
        at = pl.ds(start, rows)
        copies.append((at, pltpu.make_async_copy(spectra.at[pl.ds(first + start, rows)], stage.at[at], sems.at[i])))
        start += rows
    return copies


def load_kernel(sizes, spectra, basis, loadings, near_basis, near_loadings, high, low, stage, sems, side_sems):
    copies = row_copies(spectra, stage, sems, 0, sizes)
    sides = [
        pltpu.make_async_copy(basis, near_basis, side_sems.at[0]),
        pltpu.make_async_copy(loadings, near_loadings, side_sems.at[1]),
    ]
    for copy in [copy for _, copy in copies] + sides:
        copy.start()
    for at, copy in copies:
        copy.wait()
        high[at, :], low[at, :] = halves(stage[at, :])
    for copy in sides:
        copy.wait()


def numer_kernel(group, sizes, spectra, basis, partner, high, low, numer, tied, late_high, late_low, stage, sems):
    rank, cols = basis.shape
    early = high.shape[0]
    copies = row_copies(spectra, stage, sems, early, sizes)
    for _, copy in copies:
        copy.start()
    blocks = cols // LANES
    for j in range(blocks):
        mirrored = mirror_lanes(partner[:, pl.ds((blocks - 1 - j) * LANES, LANES)])
        at = pl.ds(j * LANES, LANES)
        tied[:, at] = 0.5 * (basis[:, at] + mirrored)
    tied_parts = both_halves(tied[...])

    def put(start, block_high, block_low):
        terms = dot(block_high, tied_parts, NT)
        terms = terms[:, :rank] + terms[:, rank:] + dot(block_low, tied_parts[:rank], NT)
        numer[:, pl.ds(start, block_high.shape[0])] = terms.T

    def turn(start, block_high, block_low):
        terms = dot(tied_parts, block_high, NT)
        numer[:, pl.ds(start, block_high.shape[0])] = (
            terms[:rank] + terms[rank:] + dot(tied_parts[:rank], block_low, NT)
        )

    for start in range(0, early, group):
        at = pl.ds(start, min(group, early - start))
        (turn if start // group % 2 == 1 else put)(start, high[at, :], low[at, :])
    for whole, copy in copies:
        copy.wait()
        late_high[whole, :], late_low[whole, :] = halves(stage[whole, :])
        size = whole.size // 2
        for i, step in enumerate((put, turn)):
            at = pl.ds(whole.start + i * size, size)
            step(early + at.start, late_high[at, :], late_low[at, :])


def ratio_kernel(tied, loadings, ratio):
    gram = 2.0 * dot(tied[...], tied[...], NT, HIGHEST)
    ratio[...] = loadings[...] / dot(gram, loadings[...], NN, HIGHEST)


def column_terms(new, high, low, late_high, late_low, at):
    rank, early = new.shape[0], high.shape[0]
    parts = both_halves(new)
    terms = dot(parts[:, :early], high[:, at], NN) + dot(parts[:, early:], late_high[:, at], NN)
    rest = dot(parts[:rank, :early], low[:, at], NN) + dot(parts[:rank, early:], late_low[:, at], NN)
    return terms[:rank] + terms[rank:] + rest


def odd_chip():
    count = lax.axis_size("scan")
    index = lax.axis_index("scan")
    ones = sum(index // (1 << bit) % 2 for bit in range(scan_steps()))
    return ones % 2 if count == 1 << scan_steps() else index * 0


def scan_steps():
    return lax.axis_size("scan").bit_length() - 1


def place(block, blocks, turned):
    return block + turned * (blocks - 1 - 2 * block)


def maybe_mirror(block, turned):
    lane = lax.broadcasted_iota(jnp.int32, block.shape, 1)
    return jnp.take_along_axis(block, place(lane, LANES, turned), axis=1, mode="promise_in_bounds")


def half_terms(width, new, arrays, turned, first, out):
    rank, cols = new.shape[0], arrays[0].shape[1]
    half, last = cols // 2, first + out.shape[0] // rank
    wide = width // LANES
    for block in range(first, last, wide):
        group = min(wide, last - block)
        start = block * LANES + turned * (half + (half // LANES - 2 * block - group) * LANES)
        terms = column_terms(new, *arrays, pl.ds(pl.multiple_of(start, LANES), group * LANES))
        for b in range(group):
            row = (block - first + place(b, group, turned)) * rank
            part = maybe_mirror(terms[:, b * LANES:(b + 1) * LANES], turned)
            out[pl.ds(pl.multiple_of(row, rank), rank), :] = part


def send_kernel(width, own, other, ratio, high, low, late_high, late_low, send):
    new = ratio[...] * (own[...] + other[...])
    half_terms(width, new, (high, low, late_high, late_low), 1 - odd_chip(), 0, send)


def keep_kernel(width, own, other, ratio, high, low, late_high, late_low, new_loadings, keep, cross, stage, sem):
    rank = own.shape[0]
    new = ratio[...] * (own[...] + other[...])
    stage[...] = new
    copy = pltpu.make_async_copy(stage, new_loadings, sem)
    copy.start()
    square = dot(new, new, NT, HIGHEST)
    per_row = LANES // rank
    strip = rank // per_row
    cross[...] = jnp.concatenate([square[i * strip:(i + 1) * strip] for i in range(per_row)], axis=1)
    half_terms(width, new, (high, low, late_high, late_low), odd_chip(), 0, keep)
    copy.wait()


def piece_start(turned, first, count, blocks):
    return pl.multiple_of((first + turned * (2 * blocks - 2 * first - count)) * LANES, LANES)


def basis_piece(tied, scale, numers, turned, first, out):
    rank, cols = tied.shape
    count = numers.shape[0] // rank
    start = piece_start(turned, first, count, cols // 2 // LANES)
    for block in range(count):
        numer = maybe_mirror(numers[block * rank:(block + 1) * rank], turned)
        column = pl.multiple_of(place(block, count, turned) * LANES, LANES)
        at = pl.ds(pl.multiple_of(start + column, LANES), LANES)
        out[:, pl.ds(column, LANES)] = tied[:, at] * (0.5 * numer) / scale[:, at]


def first_kernel(tied, sums, scale, near):
    rank = tied.shape[0]
    per_row = LANES // rank
    strip = rank // per_row
    packed = sums[:strip, :]
    cross = jnp.concatenate([packed[:, i * rank:(i + 1) * rank] for i in range(per_row)], axis=0)
    scale[...] = dot(cross, tied[...], NN, HIGHEST)
    basis_piece(tied, scale, sums[strip:, :], odd_chip(), 0, near)


def middle_kernel(first, tied, scale, sums, others, near, far):
    odd = odd_chip()
    basis_piece(tied, scale, sums[...], odd, first, near)
    basis_piece(tied, scale, others[...], 1 - odd, 0, far)


def last_kernel(first, tied, scale, near, more, far, others, new_basis, rest, sems):
    cols = tied.shape[1]
    blocks = cols // 2 // LANES
    odd = odd_chip()
    copies = []
    for i, (piece, turned, begin) in enumerate(
        ((near, odd, 0), (more, odd, first), (far, 1 - odd, 0), (rest, 1 - odd, first))
    ):
        if piece is rest:
            basis_piece(tied, scale, others[...], turned, first, rest)
        width = piece.shape[1]
        start = piece_start(turned, begin, width // LANES, blocks)
        copies.append(pltpu.make_async_copy(piece, new_basis.at[:, pl.ds(start, width)], sems.at[i]))
        copies[-1].start()
    for copy in copies:
        copy.wait()


def over_det(x):
    return lax.ppermute(x, "det", [(0, 1), (1, 0)])


def stride_orders(steps):
    cuts = [round(steps * i / 3) for i in range(4)]
    groups = [list(range(a, b)) for a, b in zip(cuts, cuts[1:])]
    return [
        [sum((groups[g] for g in order), []) for order in stream]
        for stream in (((1, 0, 2), (2, 1, 0)), ((1, 2, 0), (2, 0, 1)))
    ]


def scan_sums(parts):
    count, steps = lax.axis_size("scan"), scan_steps()
    if count != 1 << steps:
        return [(total, jnp.zeros_like(total)) for total in lax.psum(parts, "scan")]
    orders = stride_orders(steps)
    pairs = [(part, jnp.zeros_like(part)) for part in parts]
    for step in range(steps):
        received = []
        for part, order in zip(parts, orders):
            route = []
            for i in range(count):
                for core in range(2):
                    half = (core + i.bit_count()) % 2
                    route.append((2 * i + core, 2 * (i ^ 1 << order[half][step]) + 1 - core))
            received.append(lax.ppermute(part, ("scan", "det"), route))
        pairs = list(zip(parts, received))
        parts = [part + other for part, other in pairs]
    return pairs


def per_device(spectra, basis, loadings):
    positions, cols = spectra.shape
    rank = basis.shape[0]
    half = cols // 2
    early = positions // 2
    late = positions - early
    early_sizes = (early // 2, early // 4, early // 8, early // 8)
    late_sizes = (late // 2, late // 2)
    tall = half // LANES * rank
    strip = rank * rank // LANES
    product = 2 * rank * positions * cols
    dma = pltpu.SemaphoreType.DMA

    partner = over_det(basis)
    near_basis, near_loadings, high, low = call(
        functools.partial(load_kernel, early_sizes), "load",
        [(HBM, spectra), (HBM, basis), (HBM, loadings)],
        [(VMEM, basis.shape, F32), (VMEM, loadings.shape, F32), (VMEM, (early, cols), BF16), (VMEM, (early, cols), BF16)],
        [VMEM((early, cols), F32), dma((len(early_sizes),)), dma((2,))],
        moved=4 * early * cols,
    )
    numer, tied, late_high, late_low = call(
        functools.partial(numer_kernel, 128, late_sizes), "numer",
        [(HBM, spectra), (VMEM, near_basis), (VMEM, partner), (VMEM, high), (VMEM, low)],
        [(VMEM, loadings.shape, F32), (VMEM, basis.shape, F32), (VMEM, (late, cols), BF16), (VMEM, (late, cols), BF16)],
        [VMEM((late, cols), F32), dma((len(late_sizes),))],
        flops=3 * product, moved=4 * late * cols,
    )
    other = over_det(numer)
    ratio, = call(ratio_kernel, "ratio", [(VMEM, tied), (VMEM, near_loadings)], [(VMEM, loadings.shape, F32)], flops=product // 16)
    operands = [(VMEM, x) for x in (numer, other, ratio, high, low, late_high, late_low)]
    send, = call(
        functools.partial(send_kernel, 256), "send", operands, [(VMEM, (tall, LANES), F32)], flops=3 * product // 2
    )
    received = over_det(send)
    new_loadings, keep, cross = call(
        functools.partial(keep_kernel, 512), "keep", operands,
        [(HBM, loadings.shape, F32), (VMEM, (tall, LANES), F32), (VMEM, (strip, LANES), F32)],
        [VMEM(loadings.shape, F32), dma(())],
        flops=3 * product // 2,
    )
    folded = keep + received
    cut = tall // rank // 2 * rank
    parts = (jnp.concatenate([cross, folded[:cut]], axis=0), folded[cut:])
    (mine, theirs), (my_rest, their_rest) = scan_sums(lax.optimization_barrier(parts))
    sums = mine + theirs
    others = over_det(sums[strip:])
    scale, near = call(
        first_kernel, "first", [(VMEM, tied), (VMEM, sums)],
        [(VMEM, basis.shape, F32), (VMEM, (rank, cut // rank * LANES), F32)],
        flops=product // 32,
    )
    scale, near, their_rest = lax.optimization_barrier((scale, near, their_rest))
    rest = my_rest + their_rest
    other_rest = over_det(rest)
    wide = (rank, half - cut // rank * LANES)
    more, far = call(
        functools.partial(middle_kernel, cut // rank), "middle",
        [(VMEM, x) for x in (tied, scale, rest, others)],
        [(VMEM, wide, F32), (VMEM, near.shape, F32)],
        flops=product // 64,
    )
    new_basis, = call(
        functools.partial(last_kernel, cut // rank), "last",
        [(VMEM, x) for x in (tied, scale, near, more, far, other_rest)],
        [(HBM, basis.shape, F32)],
        [VMEM(wide, F32), dma((4,))],
    )
    return new_loadings, new_basis


def solution(mesh):
    in_specs = (P(("grp", "scan"), "det"), P("grp", "det"), P("grp", "scan"))
    out_specs = (P("grp", "scan"), P("grp", "det"))
    return jax.shard_map(
        per_device, mesh=mesh, in_specs=in_specs, out_specs=out_specs, check_vma=False
    )
```
